32 devices in a mesh: det: 4 (over y, core), patch: 8 (over z, x).
Axes of the slice: x: 2, y: 2, z: 4, core: 2. Of those that a mesh axis runs over, the one named last changes fastest.
Arguments:
- exposure: bfloat16 [8192, 4096], P(('det', 'patch')), may hold values from -8 to 8
- block_dest: int32 [1024], P(('det', 'patch')), may hold values from 0 to 1023, as said below
- band_offset: int32 [1024], P(('det', 'patch')), may hold values from -8 to 8
- col_shift: float32 [1024], P(('det', 'patch')), may hold values from 0.05 to 0.95
- block_weight: float32 [1024], P(('det', 'patch')), may hold values from 0.5 to 4
- basis_width: float32 [3], replicated, may hold values from 1 to 5
- kernel_fit: float32 [32, 3, 6], P(('det', 'patch')), may hold values from -3 to 3
- fit_owner: int32 [1], replicated, may hold values from 0 to 31
Outputs:
- matched: bfloat16 [8192, 4096], P(('det', 'patch'))
- coverage: float32 [1024], P(('det', 'patch'))
The draws below stay inside these ranges and needn't reach their ends.
Inputs may be any that keep to these rules, and one draw needn't show every extreme that they name: `block_dest`: block b of device d (b in d * 32 .. d * 32 + 31) lands in a slot of a device of d's det group (slots d' 32 .. d' 32 + 31 belong to device d'); no device sends more than 5 of its blocks to one device, and every device sends exactly 5 to some device.
All inputs are finite; a program needn't handle non-finite values.
Results may differ from the reference program's by a relative error of at most 0.013.
Values may be sent and summed in bfloat16 or wider, within the bound.
No kernel may reach another device: no remote copies, remote signals or barrier semaphores. Data moves between devices by JAX's collectives and lax.ppermute only.
A program may use at most 448 MiB of HBM per device.

```python
import math
import jax
import jax.numpy as jnp
from jax import lax

W = 4096
TAPS = 31
BASES = 3
NPOLY = 6
BLK = 8
BPD = 32
ROWS_DEV = 256
BLOCKS = 1024
ROWS = 8192
N_PATCH = 8
DEVICES = 32


def draw_block_dest(key, part):
    mean_count = BPD // N_PATCH
    counts = jnp.full((N_PATCH,), mean_count, jnp.int32).at[0].add(1).at[1].add(-1)

    def one_device(device_key, device_index):
        key_order, key_shuffle, key_slot = jax.random.split(device_key, 3)
        peer_order = jax.random.permutation(key_order, N_PATCH)
        peer_list = jnp.repeat(peer_order, counts, total_repeat_length=BPD)
        peer_list = jax.random.permutation(key_shuffle, peer_list)
        slot_list = jax.random.randint(key_slot, (BPD,), 0, BPD)
        group_index = device_index // N_PATCH
        return (group_index * N_PATCH + peer_list) * BPD + slot_list
    device_keys = jax.random.split(jax.random.fold_in(key, 17), DEVICES)
    routes = jax.vmap(one_device)(device_keys, jnp.arange(DEVICES))
    return routes.reshape(-1).astype(jnp.int32)


def plant(drawn, stream_key, least, largest):
    extent = drawn.shape
    index_at = [jax.random.randint(jax.random.fold_in(stream_key, axis), (), 0, extent[axis]) for axis in range(len(extent))]
    drawn = drawn.at[tuple(index_at)].set(least)
    longest = extent.index(max(extent))
    index_at[longest] = (index_at[longest] + 1) % extent[longest]
    return drawn.at[tuple(index_at)].set(largest)


def level_of(key, dims, cuts, least, largest):
    def one(dim, shards_of):
        draws = jax.random.uniform(jax.random.fold_in(jax.random.fold_in(key, 6), dim), (shards_of,), jnp.float32, least / len(cuts), largest / len(cuts))
        return jnp.repeat(jnp.exp(draws), dims[dim] // shards_of).reshape((-1,) + (1,) * (len(dims) - dim - 1))

    loudness = one(*cuts[0])
    for cut in cuts[1:]:
        loudness = loudness * one(*cut)
    return loudness


def normal_values(stream_key, dims, deviation, bound, cuts=(), dtype=jnp.bfloat16):
    loudness = level_of(stream_key, dims, cuts, -0.22, 0.18) if cuts else 1.0
    values = jax.random.normal(stream_key, dims, jnp.float32) * deviation * loudness
    return jnp.minimum(jnp.maximum(values, -bound), bound).astype(dtype)


def setup_inputs(seed: int = 0) -> dict:
    key_list = jax.random.split(jax.random.key(seed), 9)
    return {
        "exposure": normal_values(key_list[0], (ROWS, W), 1.0, 8.0, ((0, 32),)),
        "block_dest": draw_block_dest(jax.random.fold_in(key_list[8], 71), 0),
        "band_offset": plant(jax.random.randint(key_list[2], (BLOCKS,), -8, 9), jax.random.fold_in(key_list[2], 1), -8, 8).astype(jnp.int32),
        "col_shift": jnp.clip(0.05 + 0.9 * jax.random.uniform(key_list[3], (BLOCKS,), jnp.float32) ** level_of(key_list[3], (BLOCKS,), ((0, 32),), -0.2, 0.2), 0.05, 0.95),
        "block_weight": jnp.clip(jnp.exp(math.log(4.0) - 2.0794415 * jax.random.uniform(key_list[4], (BLOCKS,), jnp.float32) ** level_of(key_list[4], (BLOCKS,), ((0, 32),), -0.2, 0.2)), 0.5, 4.0),
        "basis_width": jnp.clip(jnp.exp(jax.random.uniform(key_list[5], (BASES,), jnp.float32, math.log(1.0), math.log(5.0))), 1.0, 5.0),
        "kernel_fit": normal_values(key_list[6], (DEVICES, BASES, NPOLY), 0.5, 3.0, ((0, 32),), jnp.float32),
        "fit_owner": jax.random.randint(key_list[7], (1,), 0, DEVICES).astype(jnp.int32),
    }


def lanczos(position):
    return jnp.sinc(position) * jnp.sinc(position / 3.0)


def resample_blocks(source_rows, offsets, shifts, weights):
    col_count = source_rows.shape[2]
    column_margin = 16
    padded = jnp.pad(source_rows, ((0, 0), (0, 0), (column_margin, column_margin)))
    summed = jnp.zeros(source_rows.shape, jnp.float32)
    for offset_tap in range(-2, 4):
        coeffs = lanczos(offset_tap - shifts)
        starts = (offsets + offset_tap + column_margin).astype(jnp.int32)
        picked = jax.vmap(lambda source_block, start_col: lax.dynamic_slice_in_dim(source_block, start_col, col_count, 1))(padded, starts)
        summed = summed + coeffs[:, None, None] * picked.astype(jnp.float32)
    return summed * weights[:, None, None]


def gaussian_taps(basis_width):
    half_span = (TAPS - 1) // 2
    positions = jnp.arange(TAPS).astype(jnp.float32) - half_span
    profile = jnp.exp(-(positions[None, :] ** 2) / (2.0 * basis_width[:, None] ** 2))
    return profile / jnp.sum(profile, axis=1, keepdims=True)


def poly_field(coeff_row, row_pos, col_pos):
    yy_pos = row_pos[:, None]
    xx_pos = col_pos[None, :]
    return (coeff_row[0] + coeff_row[1] * xx_pos + coeff_row[2] * yy_pos + coeff_row[3] * xx_pos * xx_pos
            + coeff_row[4] * xx_pos * yy_pos + coeff_row[5] * yy_pos * yy_pos)


def reference(exposure, block_dest, band_offset, col_shift, block_weight, basis_width, kernel_fit, fit_owner):
    source_blocks = exposure.reshape(BLOCKS, BLK, W)
    weighted = resample_blocks(source_blocks, band_offset, col_shift, block_weight).astype(jnp.bfloat16)
    coadd_sum = jax.ops.segment_sum(weighted.astype(jnp.float32), block_dest, num_segments=BLOCKS)
    coverage = jax.ops.segment_sum(block_weight, block_dest, num_segments=BLOCKS)
    image = (coadd_sum / jnp.maximum(coverage, 1.0)[:, None, None]).astype(jnp.bfloat16).reshape(ROWS, W)
    profile = gaussian_taps(basis_width)
    col_taps = profile.astype(jnp.bfloat16).astype(jnp.float32)
    coeff = lax.dynamic_index_in_dim(kernel_fit, fit_owner[0], 0, keepdims=False)
    half_span = (TAPS - 1) // 2
    padded_image = jnp.pad(image, ((half_span, half_span), (half_span, half_span)))
    col_pos = 2.0 * jnp.arange(W).astype(jnp.float32) / (W - 1) - 1.0

    def one_stripe(stripe_index):
        start_row = stripe_index * ROWS_DEV
        window = lax.dynamic_slice_in_dim(padded_image, start_row, ROWS_DEV + 2 * half_span, 0).astype(jnp.float32)
        row_pos = 2.0 * (start_row + jnp.arange(ROWS_DEV)).astype(jnp.float32) / (ROWS - 1) - 1.0
        result = jnp.zeros((ROWS_DEV, W), jnp.float32)
        for basis_index in range(BASES):
            colconv = jnp.zeros((ROWS_DEV + 2 * half_span, W), jnp.float32)
            for tap_index in range(TAPS):
                colconv = colconv + col_taps[basis_index, tap_index] * window[:, tap_index:tap_index + W]
            rowconv = jnp.zeros((ROWS_DEV, W), jnp.float32)
            for tap_index in range(TAPS):
                rowconv = rowconv + profile[basis_index, tap_index] * colconv[tap_index:tap_index + ROWS_DEV]
            result = result + poly_field(coeff[basis_index], row_pos, col_pos) * rowconv
        return result.astype(jnp.bfloat16)

    stripes = lax.map(one_stripe, jnp.arange(DEVICES).astype(jnp.int32))
    return stripes.reshape(ROWS, W), coverage
```

```python
import functools
import math

import jax
import jax.numpy as jnp
from jax import lax
from jax.experimental import pallas as pl
from jax.experimental.pallas import tpu as pltpu
from jax.sharding import PartitionSpec as P

TAPS = 31
HALF = 15
BASES = 3
NPOLY = 6
LANE = 128
SHIFT = 16
EDGE = 16
BOTH = ("det", "patch")
BF = jnp.bfloat16
F32 = jnp.float32
MIB = 1 << 20


def dot(a, b):
    return jnp.dot(a, b, preferred_element_type=F32)


def lanczos(position):
    def sinc(v):
        at = jnp.where(v == 0.0, 1.0, math.pi * v)
        return jnp.where(v == 0.0, 1.0, jnp.sin(at) / at)

    return sinc(position) * sinc(position / 3.0)


def resample_kernel(
    peers, cap, pairs, dest_ref, off_ref, wgt_s_ref, shift_ref, wgt_v_ref, x_ref, out_ref,
    src_ref, count_ref, xf_ref, coef_ref, diff_ref,
):
    blocks, rows, width = xf_ref.shape
    tiles = width // LANE + 1
    step = pl.program_id(0)

    @pl.when(step == 0)
    def _():
        for p in range(peers):
            count_ref[p] = 0
        for q in range(peers * cap):
            src_ref[q] = -1
        for b in range(blocks):
            peer = dest_ref[b] // blocks % peers
            rank = count_ref[peer]
            src_ref[peer * cap + rank] = b
            count_ref[peer] = rank + 1
        xf_ref[...] = x_ref[...].astype(F32).reshape(blocks, rows, width)
        tap = lax.broadcasted_iota(jnp.int32, (8, blocks), 0).astype(F32) - 2.0
        coef_ref[...] = lanczos(tap - shift_ref[...]) * wgt_v_ref[...]
        diff_ref[...] = (
            lax.broadcasted_iota(jnp.int32, diff_ref.shape, 0)
            - lax.broadcasted_iota(jnp.int32, diff_ref.shape, 1)
            - (LANE - SHIFT - 2)
        )

    lane = lax.broadcasted_iota(jnp.int32, (8, LANE), 1)
    block_lane = lax.broadcasted_iota(jnp.int32, (8, blocks), 1)
    zero = jnp.zeros((2 * rows, LANE), BF)

    def one_pair(pair, carry):
        xs, bands, metas = [], [], []
        for side in range(2):
            got = src_ref[(step * pairs + pair) * 2 + side]
            valid = got >= 0
            b = jnp.maximum(got, 0)
            xs.append(xf_ref[b])
            column = jnp.sum(
                jnp.where((block_lane == b) & valid, coef_ref[...], 0.0), axis=1, keepdims=True
            )
            off = off_ref[b]
            diff = diff_ref[...] - off
            band = jnp.zeros(diff.shape, F32)
            for t in range(6):
                band = jnp.where(diff == t, column[t : t + 1, :], band)
            bands.append(band)
            slot = jnp.where(valid, dest_ref[b] % blocks, -1).astype(F32)
            weight = jnp.full((8, LANE), jnp.where(valid, wgt_s_ref[b], 0.0), F32)
            high = weight.astype(BF).astype(F32)
            mid = (weight - high).astype(BF).astype(F32)
            low = weight - high - mid
            metas.append(
                jnp.where(
                    lane == SHIFT,
                    slot,
                    jnp.where(
                        lane == SHIFT + 1,
                        high,
                        jnp.where(lane == SHIFT + 2, mid, jnp.where(lane == SHIFT + 3, low, 0.0)),
                    ),
                )
            )
        x16 = jnp.concatenate(xs, axis=0).astype(BF)
        padded = jnp.concatenate([zero, x16, zero], axis=1)
        windows = jnp.concatenate(
            [padded[:, LANE * t : LANE * (t + 2)] for t in range(tiles)], axis=0
        )
        band = jnp.concatenate(bands, axis=1).astype(BF)
        made = dot(windows, band)
        first = pl.multiple_of(pair * 2 * rows, 2 * rows)
        for t in range(tiles):
            top = made[2 * rows * t : 2 * rows * t + rows, :LANE]
            bottom = made[2 * rows * t + rows : 2 * rows * (t + 1), LANE:]
            if t == 0:
                top = jnp.where(lane < SHIFT, 0.0, top)
                bottom = jnp.where(lane < SHIFT, 0.0, bottom)
            if t == tiles - 1:
                top = jnp.where(lane < SHIFT, top, metas[0])
                bottom = jnp.where(lane < SHIFT, bottom, metas[1])
            out_ref[pl.ds(first, 2 * rows), LANE * t : LANE * (t + 1)] = jnp.concatenate(
                [top, bottom], axis=0
            ).astype(BF)
        return carry

    lax.fori_loop(0, pairs, one_pair, 0)


def resample(exposure, dest, offset, shift, weight, peers, cap):
    rows_dev, width = exposure.shape
    blocks = dest.shape[0]
    rows = rows_dev // blocks
    all_pairs = peers * cap // 2
    steps = 4
    while all_pairs % steps:
        steps -= 1
    pairs = all_pairs // steps
    smem = pl.BlockSpec(memory_space=pltpu.SMEM)
    whole = lambda shape: pl.BlockSpec(shape, lambda i: (0, 0))
    return pl.pallas_call(
        functools.partial(resample_kernel, peers, cap, pairs),
        grid=(steps,),
        in_specs=[smem, smem, smem, whole((1, blocks)), whole((1, blocks)), whole((rows_dev, width))],
        out_specs=pl.BlockSpec((pairs * 2 * rows, width + LANE), lambda i: (i, 0)),
        out_shape=jax.ShapeDtypeStruct((peers * cap * rows, width + LANE), BF),
        scratch_shapes=[
            pltpu.SMEM((peers * cap,), jnp.int32),
            pltpu.SMEM((peers,), jnp.int32),
            pltpu.VMEM((blocks, rows, width), F32),
            pltpu.VMEM((8, blocks), F32),
            pltpu.VMEM((2 * LANE, LANE), jnp.int32),
        ],
        compiler_params=pltpu.CompilerParams(vmem_limit_bytes=40 * MIB),
        name="resample",
    )(dest, offset, weight, shift.reshape(1, blocks), weight.reshape(1, blocks), exposure)


def tables_kernel(inner, width_ref, band_ref, high_ref, low_ref, edge_high_ref, edge_low_ref):
    def weights(k, shape, delta):
        u = lax.broadcasted_iota(jnp.int32, shape, 1) - lax.broadcasted_iota(jnp.int32, shape, 0)
        u = u - delta
        at = (u - HALF).astype(F32)
        value = jnp.exp(-(at * at) / (2.0 * width * width))
        return jnp.where((u >= 0) & (u < TAPS), value, 0.0)

    def put(k, value, high, low):
        top = value.astype(BF)
        high[k] = top
        low[k] = (value - top.astype(F32)).astype(BF)

    for k in range(BASES):
        width = jnp.full((8, LANE), width_ref[k], F32)[:1, :1]
        total = jnp.sum(
            jnp.where(
                lax.broadcasted_iota(jnp.int32, (1, LANE), 1) < TAPS,
                jnp.exp(
                    -((lax.broadcasted_iota(jnp.int32, (1, LANE), 1) - HALF).astype(F32) ** 2)
                    / (2.0 * width * width)
                ),
                0.0,
            ),
            axis=1,
            keepdims=True,
        )
        u = (
            lax.broadcasted_iota(jnp.int32, (2 * LANE, LANE), 0)
            - lax.broadcasted_iota(jnp.int32, (2 * LANE, LANE), 1)
            - 1
        )
        at = (u - HALF).astype(F32)
        value = jnp.exp(-(at * at) / (2.0 * width * width)) / total
        band_ref[:, LANE * k : LANE * (k + 1)] = jnp.where(
            (u >= 0) & (u < TAPS), value, 0.0
        ).astype(BF)
        put(k, weights(k, (inner, inner + 2 * EDGE), 1) / total, high_ref, low_ref)
        put(k, weights(k, (EDGE, 3 * EDGE), 1) / total, edge_high_ref, edge_low_ref)


def tables(basis_width, rows_dev):
    inner = rows_dev - 2 * EDGE
    sd = lambda *shape: jax.ShapeDtypeStruct(shape, BF)
    return pl.pallas_call(
        functools.partial(tables_kernel, inner),
        in_specs=[pl.BlockSpec(memory_space=pltpu.SMEM)],
        out_shape=[
            sd(2 * LANE, BASES * LANE),
            sd(BASES, inner, rows_dev),
            sd(BASES, inner, rows_dev),
            sd(BASES, EDGE, 3 * EDGE),
            sd(BASES, EDGE, 3 * EDGE),
        ],
        compiler_params=pltpu.CompilerParams(vmem_limit_bytes=40 * MIB),
        name="tables",
    )(basis_width)


def coadd_kernel(steps, meta_ref, x_ref, image_ref, top_ref, bottom_ref, cover_ref):
    rows_dev, chunk = image_ref.shape
    arrived = x_ref.shape[0]
    step = pl.program_id(0)
    row = lax.broadcasted_iota(jnp.int32, (arrived, rows_dev), 0)
    col = lax.broadcasted_iota(jnp.int32, (arrived, rows_dev), 1)
    meta = meta_ref[...]
    slot = meta[:, SHIFT : SHIFT + 1].astype(F32).astype(jnp.int32)
    place = jnp.where((slot == col // 8) & (row % 8 == col % 8), 1.0, 0.0).astype(BF)
    pick = lambda v: lax.dot_general(
        place, v, (((0,), (0,)), ((), ())), preferred_element_type=F32
    )
    sums = pick(meta)
    cover = (
        sums[:, SHIFT + 1 : SHIFT + 2] + sums[:, SHIFT + 2 : SHIFT + 3] + sums[:, SHIFT + 3 : SHIFT + 4]
    )
    scale = 1.0 / jnp.maximum(cover, 1.0)
    value = pick(x_ref[...]) * scale
    column = lax.broadcasted_iota(jnp.int32, (1, chunk), 1) + step * chunk
    value = jnp.where(column < steps * chunk - LANE + SHIFT, value, 0.0).astype(BF)
    image_ref[...] = value
    top_ref[...] = value[:EDGE]
    bottom_ref[...] = value[rows_dev - EDGE :]

    @pl.when(step == 0)
    def _():
        cover_ref[...] = jnp.broadcast_to(cover, (rows_dev, LANE))


def coadd(arrived, rows_dev):
    count, width = arrived.shape
    steps = 3
    chunk = width // steps
    last = width // LANE - 1
    return pl.pallas_call(
        functools.partial(coadd_kernel, steps),
        grid=(steps,),
        in_specs=[
            pl.BlockSpec((count, LANE), lambda i: (0, last)),
            pl.BlockSpec((count, chunk), lambda i: (0, i)),
        ],
        out_specs=[
            pl.BlockSpec((rows_dev, chunk), lambda i: (0, i)),
            pl.BlockSpec((EDGE, chunk), lambda i: (0, i)),
            pl.BlockSpec((EDGE, chunk), lambda i: (0, i)),
            pl.BlockSpec((rows_dev, LANE), lambda i: (0, 0)),
        ],
        out_shape=[
            jax.ShapeDtypeStruct((rows_dev, width), BF),
            jax.ShapeDtypeStruct((EDGE, width), BF),
            jax.ShapeDtypeStruct((EDGE, width), BF),
            jax.ShapeDtypeStruct((rows_dev, LANE), F32),
        ],
        compiler_params=pltpu.CompilerParams(vmem_limit_bytes=40 * MIB),
        name="coadd",
    )(arrived, arrived)


def match_columns(x, high, low, band, fit_ref, y, first_col, col_count):
    parts = [dot(x[:, LANE * i : LANE * (i + 2)], band) for i in range(2)]
    xx = (first_col + lax.broadcasted_iota(jnp.int32, (1, 2 * LANE), 1)).astype(F32)
    xx = 2.0 * xx / (col_count - 1) - 1.0
    total = None
    for k in range(BASES):
        smooth = jnp.concatenate([p[:, LANE * k : LANE * (k + 1)] for p in parts], axis=1).astype(BF)
        both = dot(high[k], smooth) + dot(low[k], smooth)
        c = lambda i: fit_ref[k, i]
        field = (c(0) + c(2) * y + c(5) * y * y) + (c(1) + c(4) * y) * xx + c(3) * (xx * xx)
        total = field * both if total is None else total + field * both
    return total.astype(BF)


def row_position(base, count, all_rows):
    at = (base + lax.broadcasted_iota(jnp.int32, (count, 1), 0)).astype(F32)
    return 2.0 * at / (all_rows - 1) - 1.0


def inner_kernel(
    all_rows, col_count, start_ref, fit_ref, x_ref, next_ref, band_ref, high_ref, low_ref, out_ref
):
    rows_dev, chunk = out_ref.shape
    inner = rows_dev - 2 * EDGE
    step = pl.program_id(0)
    y = row_position(start_ref[0] + EDGE, inner, all_rows)
    x = jnp.concatenate([x_ref[...], next_ref[...]], axis=1)
    for g in range(chunk // (2 * LANE)):
        out_ref[EDGE : EDGE + inner, 2 * LANE * g : 2 * LANE * (g + 1)] = match_columns(
            x[:, 2 * LANE * g : 2 * LANE * g + 3 * LANE], high_ref, low_ref, band_ref[...], fit_ref, y,
            step * chunk + 2 * LANE * g, col_count,
        )


def edge_kernel(
    all_rows, col_count, rows_dev, start_ref, fit_ref, above_ref, top_ref, bottom_ref, below_ref,
    band_ref, high_ref, low_ref, old_ref, out_ref,
):
    side = pl.program_id(0)
    first = start_ref[0] + side * (rows_dev - EDGE)
    y = row_position(first, EDGE, all_rows)
    lower = side == 1
    for g in range(col_count // (2 * LANE)):
        cols = slice(2 * LANE * g, 2 * LANE * g + 3 * LANE)
        upper_rows = jnp.concatenate([above_ref[:, cols], top_ref[:, cols]], axis=0)
        lower_rows = jnp.concatenate([bottom_ref[:, cols], below_ref[:, cols]], axis=0)
        x = jnp.where(lower, lower_rows, upper_rows)
        out_ref[:, 2 * LANE * g : 2 * LANE * (g + 1)] = match_columns(
            x, high_ref, low_ref, band_ref[...], fit_ref, y, 2 * LANE * g, col_count
        )


def match_inner(image, start, fit, band, high, low, all_rows):
    rows_dev, width = image.shape
    col_count = width - LANE
    chunk = 512
    inner = rows_dev - 2 * EDGE
    smem = pl.BlockSpec(memory_space=pltpu.SMEM)
    return pl.pallas_call(
        functools.partial(inner_kernel, all_rows, col_count),
        grid=(col_count // chunk,),
        in_specs=[
            smem,
            smem,
            pl.BlockSpec((rows_dev, chunk), lambda i: (0, i)),
            pl.BlockSpec((rows_dev, LANE), lambda i: (0, (i + 1) * (chunk // LANE))),
            pl.BlockSpec(band.shape, lambda i: (0, 0)),
            pl.BlockSpec(high.shape, lambda i: (0, 0, 0)),
            pl.BlockSpec(low.shape, lambda i: (0, 0, 0)),
        ],
        out_specs=pl.BlockSpec((rows_dev, chunk), lambda i: (0, i)),
        out_shape=jax.ShapeDtypeStruct((rows_dev, col_count), BF),
        compiler_params=pltpu.CompilerParams(vmem_limit_bytes=40 * MIB),
        name="match_inner",
    )(start, fit, image, image, band, high, low)


def match_edges(matched, image, above, below, start, fit, band, high, low, all_rows):
    rows_dev, width = image.shape
    col_count = width - LANE
    smem = pl.BlockSpec(memory_space=pltpu.SMEM)
    strip = lambda rows, at: pl.BlockSpec((rows, width), lambda i: (at, 0))
    return pl.pallas_call(
        functools.partial(edge_kernel, all_rows, col_count, rows_dev),
        grid=(2,),
        in_specs=[
            smem,
            smem,
            strip(EDGE, 0),
            strip(2 * EDGE, 0),
            strip(2 * EDGE, rows_dev // (2 * EDGE) - 1),
            strip(EDGE, 0),
            pl.BlockSpec(band.shape, lambda i: (0, 0)),
            pl.BlockSpec(high.shape, lambda i: (0, 0, 0)),
            pl.BlockSpec(low.shape, lambda i: (0, 0, 0)),
            pl.BlockSpec(memory_space=pl.ANY),
        ],
        out_specs=pl.BlockSpec((EDGE, col_count), lambda i: (i * (rows_dev // EDGE - 1), 0)),
        out_shape=jax.ShapeDtypeStruct(matched.shape, BF),
        input_output_aliases={9: 0},
        compiler_params=pltpu.CompilerParams(vmem_limit_bytes=40 * MIB),
        name="match_edges",
    )(start, fit, above, image, image, below, band, high, low, matched)


def cube_sum(value):
    for axis in BOTH[::-1]:
        count = lax.axis_size(axis)
        span = 1
        while span < count:
            value = value + lax.ppermute(value, axis, [(i, i ^ span) for i in range(count)])
            span *= 2
    return value


def shards(
    exposure, block_dest, band_offset, col_shift, block_weight, basis_width, kernel_fit, fit_owner
):
    rows_dev, _ = exposure.shape
    blocks = block_dest.shape[0]
    peers = lax.axis_size("patch")
    devices = lax.axis_size(BOTH)
    cap = blocks // peers + 1
    me = lax.axis_index(BOTH)
    payload = resample(exposure, block_dest, band_offset, col_shift, block_weight, peers, cap)
    arrived = lax.all_to_all(payload, "patch", split_axis=0, concat_axis=0, tiled=True)
    fit = cube_sum(jnp.where(me == fit_owner[0], kernel_fit[0], 0.0))
    band, high, low, edge_high, edge_low = tables(basis_width, rows_dev)
    image, top, bottom, cover = coadd(arrived, rows_dev)
    down = [(i, i + 1) for i in range(devices - 1)]
    up = [(i + 1, i) for i in range(devices - 1)]
    above = lax.ppermute(bottom, BOTH, down)
    below = lax.ppermute(top, BOTH, up)
    start = jnp.full((1,), me * rows_dev, jnp.int32)
    all_rows = rows_dev * devices
    matched = match_inner(image, start, fit, band, high, low, all_rows)
    matched = match_edges(
        matched, image, above, below, start, fit, band, edge_high, edge_low, all_rows
    )
    coverage = cover.reshape(blocks, rows_dev // blocks, LANE)[:, 0, 0]
    return matched, coverage


def solution(mesh):
    in_specs = (
        P(BOTH, None),
        P(BOTH),
        P(BOTH),
        P(BOTH),
        P(BOTH),
        P(),
        P(BOTH, None, None),
        P(),
    )
    out_specs = (P(BOTH, None), P(BOTH))
    return jax.shard_map(shards, mesh=mesh, in_specs=in_specs, out_specs=out_specs, check_vma=False)
```

```python
import functools
import math

import jax
import jax.numpy as jnp
from jax import lax
from jax.experimental import pallas as pl
from jax.experimental.pallas import tpu as pltpu
from jax.sharding import PartitionSpec as P

TAPS = 31
HALF = 15
BASES = 3
NPOLY = 6
LANE = 128
SHIFT = 16
EDGE = 16
BOTH = ("det", "patch")
BF = jnp.bfloat16
F32 = jnp.float32
VMEM = 62 << 20
ROW0 = 96
STEPS1 = 4
STEPS2 = 3
CHUNK3 = 1024


def dot(a, b):
    return jnp.dot(a, b, preferred_element_type=F32)


def lanczos(position):
    def sinc(v):
        at = jnp.where(v == 0.0, 1.0, math.pi * v)
        return jnp.where(v == 0.0, 1.0, jnp.sin(at) / at)

    return sinc(position) * sinc(position / 3.0)


def resample_kernel(
    peers, cap, pairs, dest_hbm, off_hbm, wgt_hbm, shift_hbm, wgt_row_hbm, x_hbm, out_ref,
    dest_ref, off_ref, wgt_s_ref, src_ref, count_ref, shift_ref, wgt_v_ref, x_ref, xf_ref, coef_ref,
    diff_ref, sems,
):
    blocks, rows, width = xf_ref.shape
    tiles = width // LANE + 1
    step = pl.program_id(0)

    @pl.when(step == 0)
    def _():
        copies = [
            pltpu.make_async_copy(source, target, sems.at[i])
            for i, (source, target) in enumerate(
                [
                    (dest_hbm, dest_ref),
                    (off_hbm, off_ref),
                    (wgt_hbm, wgt_s_ref),
                    (shift_hbm, shift_ref),
                    (wgt_row_hbm, wgt_v_ref),
                    (x_hbm, x_ref),
                ]
            )
        ]
        for copy in copies:
            copy.start()
        diff_ref[...] = (
            lax.broadcasted_iota(jnp.int32, diff_ref.shape, 0)
            - lax.broadcasted_iota(jnp.int32, diff_ref.shape, 1)
            + (ROW0 - (LANE - SHIFT - 2))
        )
        for p in range(peers):
            count_ref[p] = 0
        for q in range(peers * cap):
            src_ref[q] = -1
        for copy in copies[:5]:
            copy.wait()
        for b in range(blocks):
            peer = dest_ref[b] // blocks % peers
            rank = count_ref[peer]
            src_ref[peer * cap + rank] = b
            count_ref[peer] = rank + 1
        tap = lax.broadcasted_iota(jnp.int32, (8, blocks), 0).astype(F32) - 2.0
        coef_ref[...] = lanczos(tap - shift_ref[...]) * wgt_v_ref[...]
        copies[5].wait()
        xf_ref[...] = x_ref[...].astype(F32).reshape(blocks, rows, width)

    lane = lax.broadcasted_iota(jnp.int32, (8, LANE), 1)
    block_lane = lax.broadcasted_iota(jnp.int32, (8, blocks), 1)
    zero = jnp.zeros((2 * rows, LANE), BF)

    for pair in range(pairs):
        xs, bands, metas = [], [], []
        for side in range(2):
            got = src_ref[(step * pairs + pair) * 2 + side]
            valid = got >= 0
            b = jnp.maximum(got, 0)
            xs.append(xf_ref[b])
            column = jnp.sum(
                jnp.where((block_lane == b) & valid, coef_ref[...], 0.0), axis=1, keepdims=True
            )
            diff = diff_ref[...] - off_ref[b]
            band = jnp.zeros(diff.shape, F32)
            for t in range(6):
                band = jnp.where(diff == t, column[t : t + 1, :], band)
            bands.append(band)
            slot = jnp.where(valid, dest_ref[b] % blocks, -1).astype(F32)
            weight = jnp.full((8, LANE), jnp.where(valid, wgt_s_ref[b], 0.0), F32)
            high = weight.astype(BF).astype(F32)
            mid = (weight - high).astype(BF).astype(F32)
            low = weight - high - mid
            metas.append(
                jnp.where(
                    lane == SHIFT,
                    slot,
                    jnp.where(
                        lane == SHIFT + 1,
                        high,
                        jnp.where(lane == SHIFT + 2, mid, jnp.where(lane == SHIFT + 3, low, 0.0)),
                    ),
                )
            )
        x16 = jnp.concatenate(xs, axis=0).astype(BF)
        padded = jnp.concatenate([zero, x16, zero], axis=1)
        windows = jnp.concatenate(
            [padded[:, LANE * t : LANE * (t + 2)] for t in range(tiles)], axis=0
        )
        band = jnp.concatenate(bands, axis=1).astype(BF)
        band = jnp.concatenate([jnp.zeros((ROW0, 2 * LANE), BF), band], axis=0)
        made = dot(windows, band)
        for t in range(tiles):
            top = made[2 * rows * t : 2 * rows * t + rows, :LANE]
            bottom = made[2 * rows * t + rows : 2 * rows * (t + 1), LANE:]
            if t == 0:
                top = jnp.where(lane < SHIFT, 0.0, top)
                bottom = jnp.where(lane < SHIFT, 0.0, bottom)
            if t == tiles - 1:
                top = jnp.where(lane < SHIFT, top, metas[0])
                bottom = jnp.where(lane < SHIFT, bottom, metas[1])
            out_ref[2 * rows * pair : 2 * rows * (pair + 1), LANE * t : LANE * (t + 1)] = (
                jnp.concatenate([top, bottom], axis=0).astype(BF)
            )


def resample(exposure, dest, offset, shift, weight, peers, cap):
    rows_dev, width = exposure.shape
    blocks = dest.shape[0]
    rows = rows_dev // blocks
    all_pairs = peers * cap // 2
    steps = STEPS1
    while all_pairs % steps:
        steps -= 1
    pairs = all_pairs // steps
    hbm = pl.BlockSpec(memory_space=pl.ANY)
    return pl.pallas_call(
        functools.partial(resample_kernel, peers, cap, pairs),
        grid=(steps,),
        in_specs=[hbm] * 6,
        out_specs=pl.BlockSpec((pairs * 2 * rows, width + LANE), lambda i: (i, 0)),
        out_shape=jax.ShapeDtypeStruct((peers * cap * rows, width + LANE), BF),
        scratch_shapes=[
            pltpu.SMEM((blocks,), jnp.int32),
            pltpu.SMEM((blocks,), jnp.int32),
            pltpu.SMEM((blocks,), F32),
            pltpu.SMEM((peers * cap,), jnp.int32),
            pltpu.SMEM((peers,), jnp.int32),
            pltpu.VMEM((1, blocks), F32),
            pltpu.VMEM((1, blocks), F32),
            pltpu.VMEM((rows_dev, width), BF),
            pltpu.VMEM((blocks, rows, width), F32),
            pltpu.VMEM((8, blocks), F32),
            pltpu.VMEM((2 * LANE - ROW0, LANE), jnp.int32),
            pltpu.SemaphoreType.DMA((6,)),
        ],
        compiler_params=pltpu.CompilerParams(vmem_limit_bytes=VMEM),
        name="resample",
    )(dest, offset, weight, shift.reshape(1, blocks), weight.reshape(1, blocks), exposure)


def gauss_band(shape, rows_axis, width, total):
    u = lax.broadcasted_iota(jnp.int32, shape, 1 - rows_axis)
    u = u - lax.broadcasted_iota(jnp.int32, shape, rows_axis) - 1
    at = (u - HALF).astype(F32)
    value = jnp.exp(-(at * at) / (2.0 * width * width)) / total
    return jnp.where((u >= 0) & (u < TAPS), value, 0.0).astype(BF)


def tables_kernel(width_ref, band_ref, inner_ref, edge_ref):
    inner, rows_dev = inner_ref.shape[1:]
    edge_ref[...] = jnp.zeros(edge_ref.shape, BF)
    for k in range(BASES):
        width = jnp.full((8, LANE), width_ref[k], F32)[:1, :1]
        tap = lax.broadcasted_iota(jnp.int32, (1, LANE), 1)
        at = (tap - HALF).astype(F32)
        each = jnp.where(tap < TAPS, jnp.exp(-(at * at) / (2.0 * width * width)), 0.0)
        total = jnp.sum(each, axis=1, keepdims=True)
        band_ref[:, LANE * k : LANE * (k + 1)] = gauss_band((2 * LANE, LANE), 1, width, total)
        inner_ref[k] = gauss_band((inner, rows_dev), 0, width, total)
        strip = gauss_band((EDGE, 3 * EDGE), 0, width, total)
        none = jnp.zeros(strip.shape, BF)
        edge_ref[2 * EDGE * k : 2 * EDGE * k + EDGE, :] = jnp.concatenate([strip, none], axis=1)
        edge_ref[2 * EDGE * k + EDGE : 2 * EDGE * (k + 1), :] = jnp.concatenate([none, strip], axis=1)


def tables(basis_width, rows_dev):
    sd = lambda *shape: jax.ShapeDtypeStruct(shape, BF)
    return pl.pallas_call(
        tables_kernel,
        in_specs=[pl.BlockSpec(memory_space=pltpu.SMEM)],
        out_shape=[
            sd(2 * LANE, BASES * LANE),
            sd(BASES, rows_dev - 2 * EDGE, rows_dev),
            sd(2 * EDGE * BASES, 6 * EDGE),
        ],
        compiler_params=pltpu.CompilerParams(vmem_limit_bytes=VMEM),
        name="tables",
    )(basis_width)


def coadd_kernel(
    rows, meta_ref, x_ref, image_ref, top_ref, bottom_ref, cover_ref, place_ref, scale_ref
):
    rows_dev, chunk = image_ref.shape
    arrived = x_ref.shape[0]
    slots = rows_dev // rows
    step = pl.program_id(0)

    @pl.when(step == 0)
    def _():
        meta = meta_ref[...]
        slot = meta[:, SHIFT : SHIFT + 1].astype(F32)
        across = jnp.broadcast_to(slot, (arrived, LANE)).T[:1].astype(jnp.int32)
        row = lax.broadcasted_iota(jnp.int32, (rows_dev, 1), 0)
        lane = lax.broadcasted_iota(jnp.int32, (1, arrived), 1)
        match = (across == row // rows) & (lane % rows == row % rows)
        place = jnp.where(match, 1.0, 0.0).astype(BF)
        place_ref[...] = place
        sums = dot(place, meta)
        cover = sums[:, SHIFT + 1 : SHIFT + 2] + sums[:, SHIFT + 2 : SHIFT + 3]
        cover = cover + sums[:, SHIFT + 3 : SHIFT + 4]
        scale_ref[...] = jnp.broadcast_to(1.0 / jnp.maximum(cover, 1.0), (rows_dev, LANE))
        source = lax.broadcasted_iota(jnp.int32, (arrived, 1), 0)
        index = lax.broadcasted_iota(jnp.int32, (1, slots), 1)
        match = (slot.astype(jnp.int32) == index) & (source % rows == 0)
        sums = lax.dot_general(
            meta, jnp.where(match, 1.0, 0.0).astype(BF), (((0,), (0,)), ((), ())),
            preferred_element_type=F32,
        )
        cover = sums[SHIFT + 1 : SHIFT + 2] + sums[SHIFT + 2 : SHIFT + 3]
        cover_ref[...] = cover + sums[SHIFT + 3 : SHIFT + 4]

    value = dot(place_ref[...], x_ref[...]) * scale_ref[:, :1]
    column = lax.broadcasted_iota(jnp.int32, (1, chunk), 1) + step * chunk
    tail = pl.num_programs(0) * chunk - LANE + SHIFT
    value = jnp.where(column < tail, value, 0.0).astype(BF)
    image_ref[...] = value
    top_ref[...] = value[:EDGE]
    bottom_ref[...] = value[rows_dev - EDGE :]


def coadd(arrived, rows_dev, rows):
    count, width = arrived.shape
    steps = STEPS2
    chunk = width // steps
    last = width // LANE - 1
    strip = pl.BlockSpec((EDGE, chunk), lambda i: (0, i))
    sd = jax.ShapeDtypeStruct
    return pl.pallas_call(
        functools.partial(coadd_kernel, rows),
        grid=(steps,),
        in_specs=[
            pl.BlockSpec((count, LANE), lambda i: (0, last)),
            pl.BlockSpec((count, chunk), lambda i: (0, i)),
        ],
        out_specs=[
            pl.BlockSpec((rows_dev, chunk), lambda i: (0, i)),
            strip,
            strip,
            pl.BlockSpec((1, rows_dev // rows), lambda i: (0, 0)),
        ],
        out_shape=[
            sd((rows_dev, width), BF),
            sd((EDGE, width), BF),
            sd((EDGE, width), BF),
            sd((1, rows_dev // rows), F32),
        ],
        scratch_shapes=[pltpu.VMEM((rows_dev, count), BF), pltpu.VMEM((rows_dev, LANE), F32)],
        compiler_params=pltpu.CompilerParams(vmem_limit_bytes=VMEM),
        name="coadd",
    )(arrived, arrived)


def row_position(base, count, all_rows):
    at = (base + lax.broadcasted_iota(jnp.int32, (count, 1), 0)).astype(F32)
    return 2.0 * at / (all_rows - 1) - 1.0


def col_position(first, count, col_count):
    at = (first + lax.broadcasted_iota(jnp.int32, (1, count), 1)).astype(F32)
    return 2.0 * at / (col_count - 1) - 1.0


def field(fit_ref, k, y, xx):
    c = lambda i: fit_ref[NPOLY * k + i]
    return (c(0) + c(2) * y + c(5) * y * y) + (c(1) + c(4) * y) * xx + c(3) * (xx * xx)


def tile_windows(value, tiles):
    return jnp.concatenate([value[:, LANE * t : LANE * (t + 2)] for t in range(tiles)], axis=0)


def inner_kernel(
    all_rows, col_count, start_ref, fit_ref, x_ref, next_ref, band_ref, inner_ref, out_ref
):
    rows_dev, chunk = out_ref.shape
    inner = rows_dev - 2 * EDGE
    tiles = chunk // LANE
    first = pl.program_id(0) * chunk
    image = jnp.concatenate([x_ref[...], next_ref[...]], axis=1)
    smooth = dot(tile_windows(image, tiles), band_ref[...]).astype(BF)
    y = row_position(start_ref[0] + EDGE, inner, all_rows)
    xx = col_position(first, chunk, col_count)
    total = None
    for k in range(BASES):
        part = jnp.concatenate(
            [smooth[rows_dev * t : rows_dev * (t + 1), LANE * k : LANE * (k + 1)] for t in range(tiles)],
            axis=1,
        )
        term = field(fit_ref, k, y, xx) * dot(inner_ref[k], part)
        total = term if total is None else total + term
    out_ref[EDGE : EDGE + inner, :] = total.astype(BF)


def match_inner(image, start, fit, band, inner, all_rows):
    rows_dev, width = image.shape
    col_count = width - LANE
    chunk = CHUNK3
    smem = pl.BlockSpec(memory_space=pltpu.SMEM)
    whole = lambda v: pl.BlockSpec(v.shape, lambda i: (0,) * v.ndim)
    return pl.pallas_call(
        functools.partial(inner_kernel, all_rows, col_count),
        grid=(col_count // chunk,),
        in_specs=[
            smem,
            smem,
            pl.BlockSpec((rows_dev, chunk), lambda i: (0, i)),
            pl.BlockSpec((rows_dev, LANE), lambda i: (0, (i + 1) * (chunk // LANE))),
            whole(band),
            whole(inner),
        ],
        out_specs=pl.BlockSpec((rows_dev, chunk), lambda i: (0, i)),
        out_shape=jax.ShapeDtypeStruct((rows_dev, col_count), BF),
        compiler_params=pltpu.CompilerParams(vmem_limit_bytes=VMEM),
        name="match_inner",
    )(start, fit, image, image, band, inner)


def edge_kernel(
    all_rows, rows_dev, start_ref, fit_ref, above_ref, top_ref, bottom_ref, below_ref, band_ref, edge_ref, old_ref, out_ref, made_ref, sems,
):
    col_count = made_ref.shape[1]
    tiles = col_count // LANE
    strips_in = (above_ref, top_ref, bottom_ref, below_ref)
    x = jnp.concatenate([ref[...] for ref in strips_in], axis=0)
    rowconv = dot(edge_ref[...], x).astype(BF)
    y = jnp.concatenate(
        [row_position(start_ref[0] + at, EDGE, all_rows) for at in (0, rows_dev - EDGE)], axis=0
    )
    both = 2 * EDGE
    parts = [
        dot(tile_windows(rowconv[both * k : both * (k + 1)], tiles), band_ref[:, LANE * k : LANE * (k + 1)])
        for k in range(BASES)
    ]
    for t in range(tiles):
        xx = col_position(LANE * t, LANE, col_count)
        total = None
        for k in range(BASES):
            term = field(fit_ref, k, y, xx) * parts[k][both * t : both * (t + 1)]
            total = term if total is None else total + term
        made_ref[:, LANE * t : LANE * (t + 1)] = total.astype(BF)
    copies = [
        pltpu.make_async_copy(
            made_ref.at[pl.ds(EDGE * i, EDGE)], out_ref.at[pl.ds(at, EDGE)], sems.at[i]
        )
        for i, at in enumerate((0, rows_dev - EDGE))
    ]
    for copy in copies:
        copy.start()
    for copy in copies:
        copy.wait()


def match_edges(matched, image, above, below, start, fit, band, edge, all_rows):
    rows_dev, col_count = matched.shape
    width = image.shape[1]
    smem = pl.BlockSpec(memory_space=pltpu.SMEM)
    hbm = pl.BlockSpec(memory_space=pl.ANY)
    block = lambda rows, cols, at: pl.BlockSpec((rows, cols), lambda i: (at, 0))
    return pl.pallas_call(
        functools.partial(edge_kernel, all_rows, rows_dev),
        grid=(1,),
        in_specs=[
            smem,
            smem,
            block(EDGE, width, 0),
            block(2 * EDGE, width, 0),
            block(2 * EDGE, width, rows_dev // (2 * EDGE) - 1),
            block(EDGE, width, 0),
            block(*band.shape, 0),
            block(*edge.shape, 0),
            hbm,
        ],
        out_specs=hbm,
        out_shape=jax.ShapeDtypeStruct(matched.shape, BF),
        scratch_shapes=[pltpu.VMEM((2 * EDGE, col_count), BF), pltpu.SemaphoreType.DMA((2,))],
        input_output_aliases={8: 0},
        compiler_params=pltpu.CompilerParams(vmem_limit_bytes=VMEM),
        name="match_edges",
    )(start, fit, above, image, image, below, band, edge, matched)


def axis_sum(value, axis):
    count = lax.axis_size(axis)
    span = 1
    while span < count:
        value = value + lax.ppermute(value, axis, [(i, i ^ span) for i in range(count)])
        span *= 2
    return value


def shards(
    exposure, block_dest, band_offset, col_shift, block_weight, basis_width, kernel_fit, fit_owner
):
    rows_dev, _ = exposure.shape
    blocks = block_dest.shape[0]
    peers = lax.axis_size("patch")
    devices = lax.axis_size(BOTH)
    cap = blocks // peers + 1
    me = lax.axis_index(BOTH)
    payload = resample(exposure, block_dest, band_offset, col_shift, block_weight, peers, cap)
    arrived = lax.all_to_all(payload, "patch", split_axis=0, concat_axis=0, tiled=True)
    fit = jnp.where(me == fit_owner[0], kernel_fit[0], 0.0).reshape(1, BASES * NPOLY)
    band, inner, edge = tables(basis_width, rows_dev)
    payload, fit = lax.optimization_barrier((payload, fit))
    fit = axis_sum(fit, "det")
    fit, band, inner, edge = lax.optimization_barrier((fit, band, inner, edge))
    fit = axis_sum(fit, "patch")
    arrived, fit = lax.optimization_barrier((arrived, fit))
    fit = fit.reshape(BASES * NPOLY)
    image, top, bottom, cover = coadd(arrived, rows_dev, rows_dev // blocks)
    down = [(i, i + 1) for i in range(devices - 1)]
    up = [(i + 1, i) for i in range(devices - 1)]
    above = lax.ppermute(bottom, BOTH, down)
    below = lax.ppermute(top, BOTH, up)
    start = jnp.full((1,), me * rows_dev, jnp.int32)
    all_rows = rows_dev * devices
    matched = match_inner(image, start, fit, band, inner, all_rows)
    matched = match_edges(matched, image, above, below, start, fit, band, edge, all_rows)
    return matched, cover.reshape(blocks)


def solution(mesh):
    in_specs = (
        P(BOTH, None),
        P(BOTH),
        P(BOTH),
        P(BOTH),
        P(BOTH),
        P(),
        P(BOTH, None, None),
        P(),
    )
    out_specs = (P(BOTH, None), P(BOTH))
    return jax.shard_map(shards, mesh=mesh, in_specs=in_specs, out_specs=out_specs, check_vma=False)
```

```python
import functools
import math

import jax
import jax.numpy as jnp
from jax import lax
from jax.experimental import pallas as pl
from jax.experimental.pallas import tpu as pltpu
from jax.sharding import PartitionSpec as P

TAPS = 31
HALF = 15
BASES = 3
NPOLY = 6
LANE = 128
SHIFT = 16
EDGE = 16
BOTH = ("det", "patch")
BF = jnp.bfloat16
F32 = jnp.float32
MIB = 1 << 20
EARLY_VMEM, LATE_VMEM = 62 * MIB, 32 * MIB
SMALL_VMEM, MATCH_VMEM = 24 * MIB, 32 * MIB
ROW0 = 96
FIT0 = 32
CHUNK2 = 1024
CHUNK3 = 1024


def dot(a, b):
    return jnp.dot(a, b, preferred_element_type=F32)


def lanczos(position):
    def sinc(v):
        at = jnp.where(v == 0.0, 1.0, math.pi * v)
        return jnp.where(v == 0.0, 1.0, jnp.sin(at) / at)

    return sinc(position) * sinc(position / 3.0)


def resample_kernel(cap, peers, order, with_fit, *refs):
    dest_hbm, off_hbm, shift_hbm, wgt_hbm, x_hbm = refs[:5]
    outs = refs[5 + with_fit : -12]
    (
        dest_ref, off_ref, src_ref, count_ref, shift_ref, wgt_ref, x_ref, xf_ref, made_ref, diff_ref,
        fit_ref, sems,
    ) = refs[-12:]
    blocks, rows, width = xf_ref.shape
    tiles = width // LANE
    me = lax.axis_index("patch")
    smalls = [(dest_hbm, dest_ref), (off_hbm, off_ref), (shift_hbm, shift_ref), (wgt_hbm, wgt_ref)]
    if with_fit:
        smalls.append((refs[5], fit_ref))
    copies = [
        pltpu.make_async_copy(source, target, sems.at[i])
        for i, (source, target) in enumerate([(x_hbm, x_ref)] + smalls)
    ]
    for copy in copies:
        copy.start()
    diff_ref[...] = (
        lax.broadcasted_iota(jnp.int32, diff_ref.shape, 0)
        - lax.broadcasted_iota(jnp.int32, diff_ref.shape, 1)
        + (ROW0 - (LANE - SHIFT - 2))
    )
    for p in range(peers):
        count_ref[p] = 0
    for q in range(peers * cap):
        src_ref[q] = -1
    for copy in copies[1:]:
        copy.wait()
    for b in range(blocks):
        group = (dest_ref[b] // blocks % peers - me + peers) % peers
        rank = count_ref[group]
        src_ref[group * cap + rank] = b
        count_ref[group] = rank + 1
    tap = lax.broadcasted_iota(jnp.int32, (8, blocks), 0).astype(F32) - 2.0
    coefs = lanczos(tap - shift_ref[...]) * wgt_ref[...]
    lane = lax.broadcasted_iota(jnp.int32, (rows, LANE), 1)
    block_lane = lax.broadcasted_iota(jnp.int32, (8, blocks), 1)
    zero = jnp.zeros((2 * rows, LANE), BF)

    def three(value):
        high = value.astype(BF).astype(F32)
        mid = (value - high).astype(BF).astype(F32)
        return high, mid, value - high - mid

    fit_note = jnp.zeros((rows, LANE), F32)
    line = lax.broadcasted_iota(jnp.int32, (rows, LANE), 0)
    if with_fit:
        for i, part in enumerate(three(jnp.broadcast_to(fit_ref[...], (rows, LANE)))):
            fit_note = jnp.where(line == i, part, fit_note)
    copies[0].wait()
    xf_ref[...] = x_ref[...].astype(F32).reshape(blocks, rows, width)

    def one_pair(slots):
        xs, bands, notes = [], [], []
        for group, rank in slots:
            got = src_ref[group * cap + rank]
            valid = got >= 0
            b = jnp.maximum(got, 0)
            xs.append(xf_ref[b])
            own = (block_lane == b) & valid
            column = jnp.sum(jnp.where(own, coefs, 0.0), axis=1, keepdims=True)
            diff = diff_ref[...] - off_ref[b]
            band = jnp.zeros(diff.shape, F32)
            for t in range(6):
                band = jnp.where(diff == t, column[t : t + 1, :], band)
            bands.append(band)
            slot = jnp.where(valid, dest_ref[b] % blocks, -1).astype(F32)
            weight = jnp.sum(jnp.where(own, wgt_ref[...], 0.0), axis=1, keepdims=True)
            note = jnp.where(lane == 0, slot, 0.0)
            for i, part in enumerate(three(jnp.broadcast_to(weight, (rows, LANE)))):
                note = jnp.where(lane == i + 1, part, note)
            notes.append(note + fit_note if rank == 0 else note)
        x16 = jnp.concatenate(xs, axis=0).astype(BF)
        padded = jnp.concatenate([zero, x16, zero], axis=1)
        windows = jnp.concatenate(
            [padded[:, LANE * t : LANE * (t + 2)] for t in range(tiles + 1)], axis=0
        )
        band = jnp.concatenate(bands, axis=1).astype(BF)
        band = jnp.concatenate([jnp.zeros((ROW0, 2 * LANE), BF), band], axis=0)
        made = dot(windows, band)

        def piece(i):
            at = made[2 * rows * i : 2 * rows * (i + 1)]
            return at[:rows, :LANE], at[rows:, LANE:]

        for t in range(tiles):
            top, bottom = piece(t)
            if t == 0:
                last = piece(tiles)
                top = jnp.where(lane < SHIFT, last[0], top)
                bottom = jnp.where(lane < SHIFT, last[1], bottom)
            put(slots, t, top, bottom)
        put(slots, tiles, notes[0], notes[1])

    def put(slots, t, top, bottom):
        cols = slice(LANE * t, LANE * (t + 1))
        (group0, rank0), (group1, rank1) = slots
        group0, group1 = order.index(group0), order.index(group1)
        if group0 == group1:
            made_ref[group0, rows * rank0 : rows * (rank0 + 2), cols] = jnp.concatenate(
                [top, bottom], axis=0
            ).astype(BF)
        else:
            made_ref[group0, rows * rank0 : rows * (rank0 + 1), cols] = top.astype(BF)
            made_ref[group1, rows * rank1 : rows * (rank1 + 1), cols] = bottom.astype(BF)

    sends = [pltpu.make_async_copy(made_ref.at[i], outs[i], sems.at[6 + i]) for i in range(len(order))]
    for at in range(0, len(order), 2):
        two = order[at : at + 2]
        for group in two:
            for rank in range(0, cap - 1, 2):
                one_pair([(group, rank), (group, rank + 1)])
        if cap % 2:
            one_pair([(two[0], cap - 1), (two[1], cap - 1)])
        for i in range(2):
            sends[at + i].start()
    for send in sends:
        send.wait()


def resample(exposure, dest, offset, shift, weight, fit, peers, cap, order):
    rows_dev, width = exposure.shape
    blocks = dest.shape[0]
    rows = rows_dev // blocks
    hbm = pl.BlockSpec(memory_space=pl.ANY)
    return pl.pallas_call(
        functools.partial(resample_kernel, cap, peers, order, len(fit)),
        in_specs=[hbm] * (5 + len(fit)),
        out_specs=[hbm] * len(order),
        out_shape=[jax.ShapeDtypeStruct((cap * rows, width + LANE), BF)] * len(order),
        scratch_shapes=[
            pltpu.SMEM((blocks,), jnp.int32),
            pltpu.SMEM((blocks,), jnp.int32),
            pltpu.SMEM((peers * cap,), jnp.int32),
            pltpu.SMEM((peers,), jnp.int32),
            pltpu.VMEM((1, blocks), F32),
            pltpu.VMEM((1, blocks), F32),
            pltpu.VMEM((rows_dev, width), BF),
            pltpu.VMEM((blocks, rows, width), F32),
            pltpu.VMEM((len(order), cap * rows, width + LANE), BF),
            pltpu.VMEM((2 * LANE - ROW0, LANE), jnp.int32),
            pltpu.VMEM((1, LANE), F32),
            pltpu.SemaphoreType.DMA((6 + len(order),)),
        ],
        compiler_params=pltpu.CompilerParams(vmem_limit_bytes=LATE_VMEM if fit else EARLY_VMEM),
        name="resample",
    )(dest, offset, shift.reshape(1, blocks), weight.reshape(1, blocks), exposure, *fit)


def gauss_band(shape, rows_axis, width, total):
    u = lax.broadcasted_iota(jnp.int32, shape, 1 - rows_axis)
    u = u - lax.broadcasted_iota(jnp.int32, shape, rows_axis) - 1
    at = (u - HALF).astype(F32)
    value = jnp.exp(-(at * at) / (2.0 * width * width)) / total
    return jnp.where((u >= 0) & (u < TAPS), value, 0.0).astype(BF)


def tables_kernel(width_ref, band_ref, inner_ref, edge_ref):
    inner, rows_dev = inner_ref.shape[1:]
    edge_ref[...] = jnp.zeros(edge_ref.shape, BF)
    for k in range(BASES):
        width = jnp.full((8, LANE), width_ref[k], F32)[:1, :1]
        tap = lax.broadcasted_iota(jnp.int32, (1, LANE), 1)
        at = (tap - HALF).astype(F32)
        each = jnp.where(tap < TAPS, jnp.exp(-(at * at) / (2.0 * width * width)), 0.0)
        total = jnp.sum(each, axis=1, keepdims=True)
        band_ref[:, LANE * k : LANE * (k + 1)] = gauss_band((2 * LANE, LANE), 1, width, total)
        inner_ref[k] = gauss_band((inner, rows_dev), 0, width, total)
        strip = gauss_band((EDGE, 3 * EDGE), 0, width, total)
        none = jnp.zeros(strip.shape, BF)
        edge_ref[2 * EDGE * k : 2 * EDGE * k + EDGE, :] = jnp.concatenate([strip, none], axis=1)
        edge_ref[2 * EDGE * k + EDGE : 2 * EDGE * (k + 1), :] = jnp.concatenate([none, strip], axis=1)


def tables(basis_width, rows_dev):
    sd = lambda *shape: jax.ShapeDtypeStruct(shape, BF)
    return pl.pallas_call(
        tables_kernel,
        in_specs=[pl.BlockSpec(memory_space=pltpu.SMEM)],
        out_shape=[
            sd(2 * LANE, BASES * LANE),
            sd(BASES, rows_dev - 2 * EDGE, rows_dev),
            sd(2 * EDGE * BASES, 6 * EDGE),
        ],
        compiler_params=pltpu.CompilerParams(vmem_limit_bytes=SMALL_VMEM),
        name="tables",
    )(basis_width)


def split_rows(groups, rows):
    even = groups[0].shape[0] // (2 * rows) * (2 * rows)
    parts = [jnp.concatenate([g[:even] for g in groups], axis=0)]
    if even < groups[0].shape[0]:
        parts.append(jnp.concatenate([g[even:].astype(F32) for g in groups], axis=0).astype(BF))
    return parts


def plan_slots(notes, rows, rows_dev):
    slots = rows_dev // rows
    fit = sum(sum(g[i : i + 1].astype(F32) for i in range(3)) for g in notes[::2])
    places, column, lined = [], None, None
    for part in split_rows(notes, rows):
        count = part.shape[0]
        slot = part[:, :1].astype(F32)
        across = jnp.broadcast_to(slot, (count, LANE)).T[:1].astype(jnp.int32)
        row = lax.broadcasted_iota(jnp.int32, (rows_dev, 1), 0)
        lane = lax.broadcasted_iota(jnp.int32, (1, count), 1)
        match = (across == row // rows) & (lane % rows == row % rows)
        place = jnp.where(match, 1.0, 0.0).astype(BF)
        sums = dot(place, part)
        column = sums if column is None else column + sums
        places.append(place)
        source = lax.broadcasted_iota(jnp.int32, (count, 1), 0)
        index = lax.broadcasted_iota(jnp.int32, (1, slots), 1)
        match = (slot.astype(jnp.int32) == index) & (source % rows == 0)
        sums = lax.dot_general(
            part, jnp.where(match, 1.0, 0.0).astype(BF), (((0,), (0,)), ((), ())),
            preferred_element_type=F32,
        )
        lined = sums if lined is None else lined + sums
    cover = column[:, 1:2] + column[:, 2:3] + column[:, 3:4]
    scale = jnp.broadcast_to(1.0 / jnp.maximum(cover, 1.0), (rows_dev, LANE))
    return places, scale, lined[1:2] + lined[2:3] + lined[3:4], fit


def coadd_kernel(peers, rows, chunk, *refs):
    groups, (image_hbm, top_ref, bottom_ref, cover_ref, fit_ref) = refs[:peers], refs[peers : peers + 5]
    x_ref, image_ref, sems = refs[peers + 5 :]
    rows_dev, width = image_ref.shape
    parts = [slice(width, width + LANE)] + [slice(i, i + chunk) for i in range(0, width, chunk)]
    copies = [
        [
            pltpu.make_async_copy(groups[g].at[:, cols], x_ref.at[g, :, cols], sems.at[i, g])
            for g in range(peers)
        ]
        for i, cols in enumerate(parts)
    ]
    for part in copies:
        for copy in part:
            copy.start()

    def arrived(i):
        for copy in copies[i]:
            copy.wait()
        return [x_ref[g, :, parts[i]] for g in range(peers)]

    places, scale, cover, fit = plan_slots(arrived(0), rows, rows_dev)
    cover_ref[...] = cover
    fit_ref[...] = fit
    sends = []
    for i, cols in enumerate(parts[1:]):
        value = None
        for part, place in zip(split_rows(arrived(i + 1), rows), places):
            sums = dot(place, part)
            value = sums if value is None else value + sums
        value = (value * scale[:, :1]).astype(BF)
        image_ref[:, cols] = value
        top_ref[:, cols] = value[:EDGE]
        bottom_ref[:, cols] = value[rows_dev - EDGE :]
        send = pltpu.make_async_copy(image_ref.at[:, cols], image_hbm.at[:, cols], sems.at[i + 1, peers])
        send.start()
        sends.append(send)
    for send in sends:
        send.wait()


def coadd(groups, rows_dev, rows):
    peers = len(groups)
    count, cols = groups[0].shape
    width = cols - LANE
    chunk = CHUNK2
    sd = jax.ShapeDtypeStruct
    hbm = pl.BlockSpec(memory_space=pl.ANY)
    vmem = pl.BlockSpec(memory_space=pltpu.VMEM)
    return pl.pallas_call(
        functools.partial(coadd_kernel, peers, rows, chunk),
        in_specs=[hbm] * peers,
        out_specs=[hbm] + [vmem] * 4,
        out_shape=[
            sd((rows_dev, width), BF),
            sd((EDGE, width), BF),
            sd((EDGE, width), BF),
            sd((1, rows_dev // rows), F32),
            sd((1, LANE), F32),
        ],
        scratch_shapes=[
            pltpu.VMEM((peers, count, cols), BF),
            pltpu.VMEM((rows_dev, width), BF),
            pltpu.SemaphoreType.DMA((1 + width // chunk, peers + 1)),
        ],
        compiler_params=pltpu.CompilerParams(vmem_limit_bytes=SMALL_VMEM),
        name="coadd",
    )(*groups)


def row_position(base, count, all_rows):
    at = (base + lax.broadcasted_iota(jnp.int32, (count, 1), 0)).astype(F32)
    return 2.0 * at / (all_rows - 1) - 1.0


def col_position(first, count, col_count):
    at = (first + lax.broadcasted_iota(jnp.int32, (1, count), 1)).astype(F32)
    return 2.0 * at / (col_count - 1) - 1.0


def field(fit_ref, k, y, xx):
    c = lambda i: fit_ref[0, FIT0 + NPOLY * k + i]
    return (c(0) + c(2) * y + c(5) * y * y) + (c(1) + c(4) * y) * xx + c(3) * (xx * xx)


def lane_of(value):
    return lax.broadcasted_iota(jnp.int32, (1, value.shape[1]), 1)


def blank(value, keep):
    return jnp.where(keep, value, jnp.zeros_like(value))


def tile_windows(value, tiles):
    return jnp.concatenate([value[:, LANE * t : LANE * (t + 2)] for t in range(tiles)], axis=0)


def inner_rows(image, first, start, fit_ref, band_ref, inner_ref, all_rows, col_count):
    rows_dev, width = image.shape
    inner = rows_dev - 2 * EDGE
    tiles = width // LANE - 1
    smooth = dot(tile_windows(image, tiles), band_ref[...]).astype(BF)
    y = row_position(start + EDGE, inner, all_rows)
    xx = col_position(first, LANE * tiles, col_count)
    total = None
    for k in range(BASES):
        part = jnp.concatenate(
            [smooth[rows_dev * t : rows_dev * (t + 1), LANE * k : LANE * (k + 1)] for t in range(tiles)],
            axis=1,
        )
        term = field(fit_ref, k, y, xx) * dot(inner_ref[k], part)
        total = term if total is None else total + term
    return total.astype(BF)


def inner_kernel(
    all_rows, col_count, start_ref, fit_ref, x_ref, next_ref, band_ref, inner_ref, out_ref
):
    rows_dev, chunk = out_ref.shape
    first = pl.program_id(0) * chunk
    x = x_ref[...]
    head = blank(x[:, :LANE], (lane_of(x[:, :LANE]) >= SHIFT) | (first > 0))
    tail = next_ref[...]
    tail = blank(tail, (lane_of(tail) < SHIFT) | (first + chunk < col_count))
    image = jnp.concatenate([head, x[:, LANE:], tail], axis=1)
    out_ref[EDGE : rows_dev - EDGE, :] = inner_rows(
        image, first, start_ref[0], fit_ref, band_ref, inner_ref, all_rows, col_count
    )


def whole_of(v):
    return pl.BlockSpec(v.shape, lambda i: (0,) * v.ndim)


def match_inner(image, start, fit, band, inner, all_rows):
    rows_dev, col_count = image.shape
    chunk = CHUNK3
    smem = pl.BlockSpec(memory_space=pltpu.SMEM)
    steps = col_count // chunk
    return pl.pallas_call(
        functools.partial(inner_kernel, all_rows, col_count),
        grid=(steps,),
        in_specs=[
            smem,
            smem,
            pl.BlockSpec((rows_dev, chunk), lambda i: (0, i)),
            pl.BlockSpec((rows_dev, LANE), lambda i: (0, (i + 1) % steps * (chunk // LANE))),
            whole_of(band),
            whole_of(inner),
        ],
        out_specs=pl.BlockSpec((rows_dev, chunk), lambda i: (0, i)),
        out_shape=jax.ShapeDtypeStruct((rows_dev, col_count), BF),
        compiler_params=pltpu.CompilerParams(vmem_limit_bytes=MATCH_VMEM),
        name="match_inner",
    )(start, fit, image, image, band, inner)


def edge_kernel(
    all_rows, rows_dev, start_ref, fit_ref, above_ref, top_ref, bottom_ref, below_ref, band_ref,
    edge_ref, old_ref, out_ref, made_ref, sems,
):
    col_count = made_ref.shape[1]
    tiles = col_count // LANE
    x = jnp.concatenate([ref[...] for ref in (above_ref, top_ref, bottom_ref, below_ref)], axis=0)
    rowconv = dot(edge_ref[...], x).astype(BF)
    head = rowconv[:, :LANE]
    rowconv = jnp.concatenate(
        [blank(head, lane_of(head) >= SHIFT), rowconv[:, LANE:], blank(head, lane_of(head) < SHIFT)],
        axis=1,
    )
    y = jnp.concatenate(
        [row_position(start_ref[0] + at, EDGE, all_rows) for at in (0, rows_dev - EDGE)], axis=0
    )
    both = 2 * EDGE
    parts = [
        dot(tile_windows(rowconv[both * k : both * (k + 1)], tiles), band_ref[:, LANE * k : LANE * (k + 1)])
        for k in range(BASES)
    ]
    for t in range(tiles):
        xx = col_position(LANE * t, LANE, col_count)
        total = None
        for k in range(BASES):
            term = field(fit_ref, k, y, xx) * parts[k][both * t : both * (t + 1)]
            total = term if total is None else total + term
        made_ref[:, LANE * t : LANE * (t + 1)] = total.astype(BF)
    copies = [
        pltpu.make_async_copy(
            made_ref.at[pl.ds(EDGE * i, EDGE)], out_ref.at[pl.ds(at, EDGE)], sems.at[i]
        )
        for i, at in enumerate((0, rows_dev - EDGE))
    ]
    for copy in copies:
        copy.start()
    for copy in copies:
        copy.wait()


def match_edges(matched, image, above, below, start, fit, band, edge, all_rows):
    rows_dev, col_count = matched.shape
    smem = pl.BlockSpec(memory_space=pltpu.SMEM)
    hbm = pl.BlockSpec(memory_space=pl.ANY)
    strip = lambda at: pl.BlockSpec((2 * EDGE, col_count), lambda i: (at, 0))
    return pl.pallas_call(
        functools.partial(edge_kernel, all_rows, rows_dev),
        grid=(1,),
        in_specs=[
            smem,
            smem,
            whole_of(above),
            strip(0),
            strip(rows_dev // (2 * EDGE) - 1),
            whole_of(below),
            whole_of(band),
            whole_of(edge),
            hbm,
        ],
        out_specs=hbm,
        out_shape=jax.ShapeDtypeStruct(matched.shape, BF),
        scratch_shapes=[pltpu.VMEM((2 * EDGE, col_count), BF), pltpu.SemaphoreType.DMA((2,))],
        input_output_aliases={8: 0},
        compiler_params=pltpu.CompilerParams(vmem_limit_bytes=SMALL_VMEM),
        name="match_edges",
    )(start, fit, above, image, image, below, band, edge, matched)


def shards(
    exposure, block_dest, band_offset, col_shift, block_weight, basis_width, kernel_fit, fit_owner
):
    rows_dev, _ = exposure.shape
    blocks = block_dest.shape[0]
    peers = lax.axis_size("patch")
    dets = lax.axis_size("det")
    devices = lax.axis_size(BOTH)
    cap = blocks // peers + 1
    me = lax.axis_index(BOTH)
    all_rows = rows_dev * devices
    start = jnp.full((1,), me * rows_dev, jnp.int32)
    send = lambda group, s: lax.ppermute(
        group, "patch", [(i, (i + s) % peers) for i in range(peers)]
    )
    order = sorted(range(peers), key=lambda s: (s % 2 == 0, -min(s, peers - s)))
    early_order = order[:2]
    late_order = sorted(order[2:], key=lambda s: -min(s, peers - s))
    partner_fit = lax.ppermute(kernel_fit, "patch", [(i, i ^ 1) for i in range(peers)])
    source = (exposure, block_dest, band_offset, col_shift, block_weight)
    early = resample(*source, [], peers, cap, early_order)
    groups = {s: send(group, s) for s, group in zip(early_order, early)}
    source, early, fit, partner_fit = lax.optimization_barrier(
        (source, early, kernel_fit, partner_fit)
    )
    owner = fit_owner[0]
    partner = me ^ 1
    fit = jnp.where(me == owner, fit, 0.0) + jnp.where(partner == owner, partner_fit, 0.0)
    fit = fit.reshape(1, BASES * NPOLY)
    span = 1
    while span < dets:
        fit = fit + lax.ppermute(fit, "det", [(i, i ^ span) for i in range(dets)])
        span *= 2
    fit = jnp.pad(fit, ((0, 0), (0, LANE - BASES * NPOLY)))
    fit = jnp.roll(fit, FIT0, axis=1)
    late = resample(*source, [fit], peers, cap, late_order)
    for s, group in zip(late_order, late):
        groups[s] = send(group, s) if s else group
    late, basis_width = lax.optimization_barrier((late, basis_width))
    band, inner, edge = tables(basis_width, rows_dev)
    groups = [groups[s] for s in range(peers)]
    groups, band, inner, edge = lax.optimization_barrier((groups, band, inner, edge))
    image, top, bottom, cover, fit = coadd(groups, rows_dev, rows_dev // blocks)
    down = [(i, i + 1) for i in range(devices - 1)]
    up = [(i + 1, i) for i in range(devices - 1)]
    above = lax.ppermute(bottom, BOTH, down)
    below = lax.ppermute(top, BOTH, up)
    matched = match_inner(image, start, fit, band, inner, all_rows)
    matched = match_edges(matched, image, above, below, start, fit, band, edge, all_rows)
    return matched, cover.reshape(blocks)


def solution(mesh):
    in_specs = (
        P(BOTH, None),
        P(BOTH),
        P(BOTH),
        P(BOTH),
        P(BOTH),
        P(),
        P(BOTH, None, None),
        P(),
    )
    out_specs = (P(BOTH, None), P(BOTH))
    return jax.shard_map(shards, mesh=mesh, in_specs=in_specs, out_specs=out_specs, check_vma=False)
```

```python
import functools
import math

import jax
import jax.numpy as jnp
from jax import lax
from jax.experimental import pallas as pl
from jax.experimental.pallas import tpu as pltpu
from jax.sharding import PartitionSpec as P

TAPS = 31
HALF = 15
BASES = 3
NPOLY = 6
LANE = 128
SHIFT = 16
EDGE = 16
BOTH = ("det", "patch")
BF = jnp.bfloat16
F32 = jnp.float32
MIB = 1 << 20
EARLY_VMEM, LATE_VMEM = 62 * MIB, 32 * MIB
SMALL_VMEM, MATCH_VMEM = 24 * MIB, 32 * MIB
ROW0 = 96
FIT0 = 32
CHUNK2 = 1024
CHUNK3 = 1024


def dot(a, b):
    return jnp.dot(a, b, preferred_element_type=F32)


def lanczos(position):
    def sinc(v):
        at = jnp.where(v == 0.0, 1.0, math.pi * v)
        return jnp.where(v == 0.0, 1.0, jnp.sin(at) / at)

    return sinc(position) * sinc(position / 3.0)


def resample_kernel(cap, peers, order, with_fit, *refs):
    dest_hbm, off_hbm, shift_hbm, wgt_hbm, x_hbm = refs[:5]
    outs = refs[5 + with_fit : -11]
    (
        dest_ref, off_ref, src_ref, count_ref, shift_ref, wgt_ref, x_ref, made_ref, diff_ref,
        fit_ref, sems,
    ) = refs[-11:]
    blocks, rows, width = x_ref.shape
    tiles = width // LANE
    me = lax.axis_index("patch")
    smalls = [(dest_hbm, dest_ref), (off_hbm, off_ref), (shift_hbm, shift_ref), (wgt_hbm, wgt_ref)]
    if with_fit:
        smalls.append((refs[5], fit_ref))
    copies = [
        pltpu.make_async_copy(source, target, sems.at[i])
        for i, (source, target) in enumerate([(x_hbm, x_ref)] + smalls)
    ]
    for copy in copies:
        copy.start()
    diff_ref[...] = (
        lax.broadcasted_iota(jnp.int32, diff_ref.shape, 0)
        - lax.broadcasted_iota(jnp.int32, diff_ref.shape, 1)
        + (ROW0 - (LANE - SHIFT - 2))
    )
    for p in range(peers):
        count_ref[p] = 0
    for q in range(peers * cap):
        src_ref[q] = -1
    for copy in copies[1:]:
        copy.wait()
    for b in range(blocks):
        group = (dest_ref[b] // blocks % peers) ^ me
        rank = count_ref[group]
        src_ref[group * cap + rank] = b
        count_ref[group] = rank + 1
    tap = lax.broadcasted_iota(jnp.int32, (8, blocks), 0).astype(F32) - 2.0
    coefs = lanczos(tap - shift_ref[...]) * wgt_ref[...]
    lane = lax.broadcasted_iota(jnp.int32, (rows, LANE), 1)
    block_lane = lax.broadcasted_iota(jnp.int32, (8, blocks), 1)
    zero = jnp.zeros((2 * rows, LANE), BF)

    def three(value):
        high = value.astype(BF).astype(F32)
        mid = (value - high).astype(BF).astype(F32)
        return high, mid, value - high - mid

    fit_note = jnp.zeros((rows, LANE), F32)
    line = lax.broadcasted_iota(jnp.int32, (rows, LANE), 0)
    if with_fit:
        for i, part in enumerate(three(jnp.broadcast_to(fit_ref[...], (rows, LANE)))):
            fit_note = jnp.where(line == i, part, fit_note)
    copies[0].wait()

    def one_pair(slots):
        xs, bands, notes = [], [], []
        for group, rank in slots:
            got = src_ref[group * cap + rank]
            valid = got >= 0
            b = jnp.maximum(got, 0)
            xs.append(x_ref[b].astype(F32))
            own = (block_lane == b) & valid
            column = jnp.sum(jnp.where(own, coefs, 0.0), axis=1, keepdims=True)
            diff = diff_ref[...] - off_ref[b]
            band = jnp.zeros(diff.shape, F32)
            for t in range(6):
                band = jnp.where(diff == t, column[t : t + 1, :], band)
            bands.append(band)
            slot = jnp.where(valid, dest_ref[b] % blocks, -1).astype(F32)
            weight = jnp.sum(jnp.where(own, wgt_ref[...], 0.0), axis=1, keepdims=True)
            note = jnp.where(lane == 0, slot, 0.0)
            for i, part in enumerate(three(jnp.broadcast_to(weight, (rows, LANE)))):
                note = jnp.where(lane == i + 1, part, note)
            notes.append(note + fit_note if rank == 0 else note)
        x16 = jnp.concatenate(xs, axis=0).astype(BF)
        padded = jnp.concatenate([zero, x16, zero], axis=1)
        windows = jnp.concatenate(
            [padded[:, LANE * t : LANE * (t + 2)] for t in range(tiles + 1)], axis=0
        )
        band = jnp.concatenate(bands, axis=1).astype(BF)
        band = jnp.concatenate([jnp.zeros((ROW0, 2 * LANE), BF), band], axis=0)
        made = dot(windows, band)

        def piece(i):
            at = made[2 * rows * i : 2 * rows * (i + 1)]
            return at[:rows, :LANE], at[rows:, LANE:]

        for t in range(tiles):
            top, bottom = piece(t)
            if t == 0:
                last = piece(tiles)
                top = jnp.where(lane < SHIFT, last[0], top)
                bottom = jnp.where(lane < SHIFT, last[1], bottom)
            put(slots, t, top, bottom)
        put(slots, tiles, notes[0], notes[1])

    def put(slots, t, top, bottom):
        cols = slice(LANE * t, LANE * (t + 1))
        (group0, rank0), (group1, rank1) = slots
        group0, group1 = order.index(group0), order.index(group1)
        if group0 == group1:
            made_ref[group0, rows * rank0 : rows * (rank0 + 2), cols] = jnp.concatenate(
                [top, bottom], axis=0
            ).astype(BF)
        else:
            made_ref[group0, rows * rank0 : rows * (rank0 + 1), cols] = top.astype(BF)
            made_ref[group1, rows * rank1 : rows * (rank1 + 1), cols] = bottom.astype(BF)

    sends = [pltpu.make_async_copy(made_ref.at[i], outs[i], sems.at[6 + i]) for i in range(len(order))]
    for at in range(0, len(order), 2):
        two = order[at : at + 2]
        for group in two:
            for rank in range(0, cap - 1, 2):
                one_pair([(group, rank), (group, rank + 1)])
        if cap % 2:
            one_pair([(two[0], cap - 1), (two[1], cap - 1)])
        for i in range(2):
            sends[at + i].start()
    for send in sends:
        send.wait()


def resample(exposure, dest, offset, shift, weight, fit, peers, cap, order):
    rows_dev, width = exposure.shape
    blocks = dest.shape[0]
    rows = rows_dev // blocks
    hbm = pl.BlockSpec(memory_space=pl.ANY)
    return pl.pallas_call(
        functools.partial(resample_kernel, cap, peers, order, len(fit)),
        in_specs=[hbm] * (5 + len(fit)),
        out_specs=[hbm] * len(order),
        out_shape=[jax.ShapeDtypeStruct((cap * rows, width + LANE), BF)] * len(order),
        scratch_shapes=[
            pltpu.SMEM((blocks,), jnp.int32),
            pltpu.SMEM((blocks,), jnp.int32),
            pltpu.SMEM((peers * cap,), jnp.int32),
            pltpu.SMEM((peers,), jnp.int32),
            pltpu.VMEM((1, blocks), F32),
            pltpu.VMEM((1, blocks), F32),
            pltpu.VMEM((blocks, rows, width), BF),
            pltpu.VMEM((len(order), cap * rows, width + LANE), BF),
            pltpu.VMEM((2 * LANE - ROW0, LANE), jnp.int32),
            pltpu.VMEM((1, LANE), F32),
            pltpu.SemaphoreType.DMA((6 + len(order),)),
        ],
        compiler_params=pltpu.CompilerParams(vmem_limit_bytes=LATE_VMEM if fit else EARLY_VMEM),
        name="resample",
    )(dest, offset, shift.reshape(1, blocks), weight.reshape(1, blocks), exposure.reshape(blocks, rows, width), *fit)


def gauss_band(shape, rows_axis, width, total):
    u = lax.broadcasted_iota(jnp.int32, shape, 1 - rows_axis)
    u = u - lax.broadcasted_iota(jnp.int32, shape, rows_axis) - 1
    at = (u - HALF).astype(F32)
    value = jnp.exp(-(at * at) / (2.0 * width * width)) / total
    return jnp.where((u >= 0) & (u < TAPS), value, 0.0).astype(BF)


def tables_kernel(width_ref, band_ref, inner_ref, edge_ref):
    inner, rows_dev = inner_ref.shape[1:]
    edge_ref[...] = jnp.zeros(edge_ref.shape, BF)
    for k in range(BASES):
        width = jnp.full((8, LANE), width_ref[k], F32)[:1, :1]
        tap = lax.broadcasted_iota(jnp.int32, (1, LANE), 1)
        at = (tap - HALF).astype(F32)
        each = jnp.where(tap < TAPS, jnp.exp(-(at * at) / (2.0 * width * width)), 0.0)
        total = jnp.sum(each, axis=1, keepdims=True)
        band_ref[:, LANE * k : LANE * (k + 1)] = gauss_band((2 * LANE, LANE), 1, width, total)
        inner_ref[k] = gauss_band((inner, rows_dev), 0, width, total)
        strip = gauss_band((EDGE, 3 * EDGE), 0, width, total)
        none = jnp.zeros(strip.shape, BF)
        edge_ref[2 * EDGE * k : 2 * EDGE * k + EDGE, :] = jnp.concatenate([strip, none], axis=1)
        edge_ref[2 * EDGE * k + EDGE : 2 * EDGE * (k + 1), :] = jnp.concatenate([none, strip], axis=1)


def tables(basis_width, rows_dev):
    sd = lambda *shape: jax.ShapeDtypeStruct(shape, BF)
    return pl.pallas_call(
        tables_kernel,
        in_specs=[pl.BlockSpec(memory_space=pltpu.SMEM)],
        out_shape=[
            sd(2 * LANE, BASES * LANE),
            sd(BASES, rows_dev - 2 * EDGE, rows_dev),
            sd(2 * EDGE * BASES, 6 * EDGE),
        ],
        compiler_params=pltpu.CompilerParams(vmem_limit_bytes=SMALL_VMEM),
        name="tables",
    )(basis_width)


def split_rows(groups, rows):
    even = groups[0].shape[0] // (2 * rows) * (2 * rows)
    parts = [jnp.concatenate([g[:even] for g in groups], axis=0)]
    if even < groups[0].shape[0]:
        parts.append(jnp.concatenate([g[even:].astype(F32) for g in groups], axis=0).astype(BF))
    return parts


def plan_slots(notes, rows, rows_dev):
    slots = rows_dev // rows
    fit = sum(sum(g[i : i + 1].astype(F32) for i in range(3)) for g in notes[::2])
    places, column, lined = [], None, None
    for part in split_rows(notes, rows):
        count = part.shape[0]
        slot = part[:, :1].astype(F32)
        across = jnp.broadcast_to(slot, (count, LANE)).T[:1].astype(jnp.int32)
        row = lax.broadcasted_iota(jnp.int32, (rows_dev, 1), 0)
        lane = lax.broadcasted_iota(jnp.int32, (1, count), 1)
        match = (across == row // rows) & (lane % rows == row % rows)
        place = jnp.where(match, 1.0, 0.0).astype(BF)
        sums = dot(place, part)
        column = sums if column is None else column + sums
        places.append(place)
        source = lax.broadcasted_iota(jnp.int32, (count, 1), 0)
        index = lax.broadcasted_iota(jnp.int32, (1, slots), 1)
        match = (slot.astype(jnp.int32) == index) & (source % rows == 0)
        sums = lax.dot_general(
            part, jnp.where(match, 1.0, 0.0).astype(BF), (((0,), (0,)), ((), ())),
            preferred_element_type=F32,
        )
        lined = sums if lined is None else lined + sums
    cover = column[:, 1:2] + column[:, 2:3] + column[:, 3:4]
    scale = jnp.broadcast_to(1.0 / jnp.maximum(cover, 1.0), (rows_dev, LANE))
    return places, scale, lined[1:2] + lined[2:3] + lined[3:4], fit


def coadd_kernel(peers, rows, chunk, *refs):
    groups, (image_hbm, inward_ref, outward_ref, cover_ref, fit_ref) = refs[:peers], refs[peers : peers + 5]
    x_ref, image_ref, sems = refs[peers + 5 :]
    odd = lax.axis_index(BOTH) % 2 == 1
    rows_dev, width = image_ref.shape
    parts = [slice(width, width + LANE)] + [slice(i, i + chunk) for i in range(0, width, chunk)]
    copies = [
        [
            pltpu.make_async_copy(groups[g].at[:, cols], x_ref.at[g, :, cols], sems.at[i, g])
            for g in range(peers)
        ]
        for i, cols in enumerate(parts)
    ]
    for part in copies:
        for copy in part:
            copy.start()

    def arrived(i):
        for copy in copies[i]:
            copy.wait()
        return [x_ref[g, :, parts[i]] for g in range(peers)]

    places, scale, cover, fit = plan_slots(arrived(0), rows, rows_dev)
    cover_ref[...] = cover
    fit_ref[...] = fit
    sends = []
    for i, cols in enumerate(parts[1:]):
        value = None
        for part, place in zip(split_rows(arrived(i + 1), rows), places):
            sums = dot(place, part)
            value = sums if value is None else value + sums
        value = (value * scale[:, :1]).astype(BF)
        image_ref[:, cols] = value
        top, bottom = value[:EDGE], value[rows_dev - EDGE :]
        inward_ref[:, cols] = jnp.where(odd, top, bottom)
        outward_ref[:, cols] = jnp.where(odd, bottom, top)
        send = pltpu.make_async_copy(image_ref.at[:, cols], image_hbm.at[:, cols], sems.at[i + 1, peers])
        send.start()
        sends.append(send)
    for send in sends:
        send.wait()


def coadd(groups, rows_dev, rows):
    peers = len(groups)
    count, cols = groups[0].shape
    width = cols - LANE
    chunk = CHUNK2
    sd = jax.ShapeDtypeStruct
    hbm = pl.BlockSpec(memory_space=pl.ANY)
    vmem = pl.BlockSpec(memory_space=pltpu.VMEM)
    return pl.pallas_call(
        functools.partial(coadd_kernel, peers, rows, chunk),
        in_specs=[hbm] * peers,
        out_specs=[hbm] + [vmem] * 4,
        out_shape=[
            sd((rows_dev, width), BF),
            sd((EDGE, width), BF),
            sd((EDGE, width), BF),
            sd((1, rows_dev // rows), F32),
            sd((1, LANE), F32),
        ],
        scratch_shapes=[
            pltpu.VMEM((peers, count, cols), BF),
            pltpu.VMEM((rows_dev, width), BF),
            pltpu.SemaphoreType.DMA((1 + width // chunk, peers + 1)),
        ],
        compiler_params=pltpu.CompilerParams(vmem_limit_bytes=SMALL_VMEM),
        name="coadd",
    )(*groups)


def row_position(base, count, all_rows):
    at = (base + lax.broadcasted_iota(jnp.int32, (count, 1), 0)).astype(F32)
    return 2.0 * at / (all_rows - 1) - 1.0


def col_position(first, count, col_count):
    at = (first + lax.broadcasted_iota(jnp.int32, (1, count), 1)).astype(F32)
    return 2.0 * at / (col_count - 1) - 1.0


def field(fit_ref, k, y, xx):
    c = lambda i: fit_ref[0, FIT0 + NPOLY * k + i]
    return (c(0) + c(2) * y + c(5) * y * y) + (c(1) + c(4) * y) * xx + c(3) * (xx * xx)


def lane_of(value):
    return lax.broadcasted_iota(jnp.int32, (1, value.shape[1]), 1)


def blank(value, keep):
    return jnp.where(keep, value, jnp.zeros_like(value))


def tile_windows(value, tiles):
    return jnp.concatenate([value[:, LANE * t : LANE * (t + 2)] for t in range(tiles)], axis=0)


def inner_rows(image, first, start, fit_ref, band_ref, inner_ref, all_rows, col_count):
    rows_dev, width = image.shape
    inner = rows_dev - 2 * EDGE
    tiles = width // LANE - 1
    smooth = dot(tile_windows(image, tiles), band_ref[...]).astype(BF)
    y = row_position(start + EDGE, inner, all_rows)
    xx = col_position(first, LANE * tiles, col_count)
    total = None
    for k in range(BASES):
        part = jnp.concatenate(
            [smooth[rows_dev * t : rows_dev * (t + 1), LANE * k : LANE * (k + 1)] for t in range(tiles)],
            axis=1,
        )
        term = field(fit_ref, k, y, xx) * dot(inner_ref[k], part)
        total = term if total is None else total + term
    return total.astype(BF)


def inner_kernel(
    all_rows, col_count, start_ref, fit_ref, x_ref, next_ref, band_ref, inner_ref, out_ref
):
    rows_dev, chunk = out_ref.shape
    first = pl.program_id(0) * chunk
    x = x_ref[...]
    head = blank(x[:, :LANE], (lane_of(x[:, :LANE]) >= SHIFT) | (first > 0))
    tail = next_ref[...]
    tail = blank(tail, (lane_of(tail) < SHIFT) | (first + chunk < col_count))
    image = jnp.concatenate([head, x[:, LANE:], tail], axis=1)
    out_ref[EDGE : rows_dev - EDGE, :] = inner_rows(
        image, first, start_ref[0], fit_ref, band_ref, inner_ref, all_rows, col_count
    )


def whole_of(v):
    return pl.BlockSpec(v.shape, lambda i: (0,) * v.ndim)


def match_inner(image, start, fit, band, inner, all_rows):
    rows_dev, col_count = image.shape
    chunk = CHUNK3
    smem = pl.BlockSpec(memory_space=pltpu.SMEM)
    steps = col_count // chunk
    return pl.pallas_call(
        functools.partial(inner_kernel, all_rows, col_count),
        grid=(steps,),
        in_specs=[
            smem,
            smem,
            pl.BlockSpec((rows_dev, chunk), lambda i: (0, i)),
            pl.BlockSpec((rows_dev, LANE), lambda i: (0, (i + 1) % steps * (chunk // LANE))),
            whole_of(band),
            whole_of(inner),
        ],
        out_specs=pl.BlockSpec((rows_dev, chunk), lambda i: (0, i)),
        out_shape=jax.ShapeDtypeStruct((rows_dev, col_count), BF),
        compiler_params=pltpu.CompilerParams(vmem_limit_bytes=MATCH_VMEM),
        name="match_inner",
    )(start, fit, image, image, band, inner)


def edge_kernel(
    all_rows, rows_dev, start_ref, fit_ref, inward_ref, top_ref, bottom_ref, outward_ref, band_ref,
    edge_ref, old_ref, out_ref, made_ref, sems,
):
    col_count = made_ref.shape[1]
    tiles = col_count // LANE
    odd = lax.axis_index(BOTH) % 2 == 1
    inward, outward = inward_ref[...], outward_ref[...]
    above, below = jnp.where(odd, inward, outward), jnp.where(odd, outward, inward)
    x = jnp.concatenate([above, top_ref[...], bottom_ref[...], below], axis=0)
    rowconv = dot(edge_ref[...], x).astype(BF)
    head = rowconv[:, :LANE]
    rowconv = jnp.concatenate(
        [blank(head, lane_of(head) >= SHIFT), rowconv[:, LANE:], blank(head, lane_of(head) < SHIFT)],
        axis=1,
    )
    y = jnp.concatenate(
        [row_position(start_ref[0] + at, EDGE, all_rows) for at in (0, rows_dev - EDGE)], axis=0
    )
    both = 2 * EDGE
    parts = [
        dot(tile_windows(rowconv[both * k : both * (k + 1)], tiles), band_ref[:, LANE * k : LANE * (k + 1)])
        for k in range(BASES)
    ]
    for t in range(tiles):
        xx = col_position(LANE * t, LANE, col_count)
        total = None
        for k in range(BASES):
            term = field(fit_ref, k, y, xx) * parts[k][both * t : both * (t + 1)]
            total = term if total is None else total + term
        made_ref[:, LANE * t : LANE * (t + 1)] = total.astype(BF)
    copies = [
        pltpu.make_async_copy(
            made_ref.at[pl.ds(EDGE * i, EDGE)], out_ref.at[pl.ds(at, EDGE)], sems.at[i]
        )
        for i, at in enumerate((0, rows_dev - EDGE))
    ]
    for copy in copies:
        copy.start()
    for copy in copies:
        copy.wait()


def match_edges(matched, image, halos, start, fit, band, edge, all_rows):
    rows_dev, col_count = matched.shape
    smem = pl.BlockSpec(memory_space=pltpu.SMEM)
    hbm = pl.BlockSpec(memory_space=pl.ANY)
    strip = lambda at: pl.BlockSpec((2 * EDGE, col_count), lambda i: (at, 0))
    return pl.pallas_call(
        functools.partial(edge_kernel, all_rows, rows_dev),
        grid=(1,),
        in_specs=[
            smem,
            smem,
            whole_of(halos[0]),
            strip(0),
            strip(rows_dev // (2 * EDGE) - 1),
            whole_of(halos[1]),
            whole_of(band),
            whole_of(edge),
            hbm,
        ],
        out_specs=hbm,
        out_shape=jax.ShapeDtypeStruct(matched.shape, BF),
        scratch_shapes=[pltpu.VMEM((2 * EDGE, col_count), BF), pltpu.SemaphoreType.DMA((2,))],
        input_output_aliases={8: 0},
        compiler_params=pltpu.CompilerParams(vmem_limit_bytes=SMALL_VMEM),
        name="match_edges",
    )(start, fit, halos[0], image, image, halos[1], band, edge, matched)


def shards(
    exposure, block_dest, band_offset, col_shift, block_weight, basis_width, kernel_fit, fit_owner
):
    rows_dev, _ = exposure.shape
    blocks = block_dest.shape[0]
    peers = lax.axis_size("patch")
    dets = lax.axis_size("det")
    devices = lax.axis_size(BOTH)
    cap = blocks // peers + 1
    me = lax.axis_index(BOTH)
    all_rows = rows_dev * devices
    start = jnp.full((1,), me * rows_dev, jnp.int32)
    send = lambda group, s: lax.ppermute(
        group, "patch", [(i, i ^ s) for i in range(peers)]
    )
    order = sorted(range(peers), key=lambda s: (s % 2 == 0, -s))
    early_order = order[:2]
    late_order = sorted(order[2:], key=lambda s: -s)
    partner_fit = lax.ppermute(kernel_fit, "patch", [(i, i ^ 1) for i in range(peers)])
    source = (exposure, block_dest, band_offset, col_shift, block_weight)
    early = resample(*source, [], peers, cap, early_order)
    groups = {s: send(group, s) for s, group in zip(early_order, early)}
    source, early, fit, partner_fit = lax.optimization_barrier(
        (source, early, kernel_fit, partner_fit)
    )
    owner = fit_owner[0]
    partner = me ^ 1
    fit = jnp.where(me == owner, fit, 0.0) + jnp.where(partner == owner, partner_fit, 0.0)
    fit = fit.reshape(1, BASES * NPOLY)
    span = 1
    while span < dets:
        fit = fit + lax.ppermute(fit, "det", [(i, i ^ span) for i in range(dets)])
        span *= 2
    fit = jnp.pad(fit, ((0, 0), (0, LANE - BASES * NPOLY)))
    fit = jnp.roll(fit, FIT0, axis=1)
    late = resample(*source, [fit], peers, cap, late_order)
    for s, group in zip(late_order, late):
        groups[s] = send(group, s) if s else group
    late, basis_width = lax.optimization_barrier((late, basis_width))
    band, inner, edge = tables(basis_width, rows_dev)
    groups = [groups[s] for s in range(peers)]
    groups, band, inner, edge = lax.optimization_barrier((groups, band, inner, edge))
    image, inward, outward, cover, fit = coadd(groups, rows_dev, rows_dev // blocks)
    even = [(i, i ^ 1) for i in range(devices)]
    odd = [(i, j) for j in range(2, devices, 2) for i, j in ((j, j - 1), (j - 1, j))]
    halos = (lax.ppermute(inward, BOTH, even), lax.ppermute(outward, BOTH, odd))
    matched = match_inner(image, start, fit, band, inner, all_rows)
    matched = match_edges(matched, image, halos, start, fit, band, edge, all_rows)
    return matched, cover.reshape(blocks)


def solution(mesh):
    in_specs = (
        P(BOTH, None),
        P(BOTH),
        P(BOTH),
        P(BOTH),
        P(BOTH),
        P(),
        P(BOTH, None, None),
        P(),
    )
    out_specs = (P(BOTH, None), P(BOTH))
    return jax.shard_map(shards, mesh=mesh, in_specs=in_specs, out_specs=out_specs, check_vma=False)
```

```python
import functools
import math

import jax
import jax.numpy as jnp
from jax import lax
from jax.experimental import pallas as pl
from jax.experimental.pallas import tpu as pltpu
from jax.sharding import PartitionSpec as P

TAPS = 31
HALF = 15
BASES = 3
NPOLY = 6
LANE = 128
SHIFT = 16
EDGE = 16
BOTH = ("det", "patch")
BF = jnp.bfloat16
F32 = jnp.float32
MIB = 1 << 20
EARLY_VMEM, LATE_VMEM = 62 * MIB, 32 * MIB
SMALL_VMEM, MATCH_VMEM = 24 * MIB, 32 * MIB
ROW0 = 96
FIT0 = 32
CHUNK2 = 2048
CHUNK3 = 2048


def dot(a, b):
    return jnp.dot(a, b, preferred_element_type=F32)


def lanczos(position):
    def sinc(v):
        at = jnp.where(v == 0.0, 1.0, math.pi * v)
        return jnp.where(v == 0.0, 1.0, jnp.sin(at) / at)

    return sinc(position) * sinc(position / 3.0)


def resample_kernel(cap, peers, order, with_fit, *refs):
    dest_hbm, off_hbm, shift_hbm, wgt_hbm, x_hbm = refs[:5]
    outs = refs[5 + with_fit : -11]
    (
        dest_ref, off_ref, src_ref, count_ref, shift_ref, wgt_ref, x_ref, made_ref, diff_ref,
        fit_ref, sems,
    ) = refs[-11:]
    blocks, rows, width = x_ref.shape
    tiles = width // LANE
    me = lax.axis_index("patch")
    smalls = [(dest_hbm, dest_ref), (off_hbm, off_ref), (shift_hbm, shift_ref), (wgt_hbm, wgt_ref)]
    if with_fit:
        smalls.append((refs[5], fit_ref))
    copies = [
        pltpu.make_async_copy(source, target, sems.at[i])
        for i, (source, target) in enumerate([(x_hbm, x_ref)] + smalls)
    ]
    for copy in copies:
        copy.start()
    diff_ref[...] = (
        lax.broadcasted_iota(jnp.int32, diff_ref.shape, 0)
        - lax.broadcasted_iota(jnp.int32, diff_ref.shape, 1)
        + (ROW0 - (LANE - SHIFT - 2))
    )
    for p in range(peers):
        count_ref[p] = 0
    for q in range(peers * cap):
        src_ref[q] = -1
    for copy in copies[1:]:
        copy.wait()
    for b in range(blocks):
        group = (dest_ref[b] // blocks % peers) ^ me
        rank = count_ref[group]
        src_ref[group * cap + rank] = b
        count_ref[group] = rank + 1
    tap = lax.broadcasted_iota(jnp.int32, (8, blocks), 0).astype(F32) - 2.0
    coefs = lanczos(tap - shift_ref[...]) * wgt_ref[...]
    lane = lax.broadcasted_iota(jnp.int32, (rows, LANE), 1)
    block_lane = lax.broadcasted_iota(jnp.int32, (8, blocks), 1)
    zero = jnp.zeros((2 * rows, LANE), BF)

    def three(value):
        high = value.astype(BF).astype(F32)
        mid = (value - high).astype(BF).astype(F32)
        return high, mid, value - high - mid

    fit_note = jnp.zeros((rows, LANE), F32)
    line = lax.broadcasted_iota(jnp.int32, (rows, LANE), 0)
    if with_fit:
        for i, part in enumerate(three(jnp.broadcast_to(fit_ref[...], (rows, LANE)))):
            fit_note = jnp.where(line == i, part, fit_note)
    copies[0].wait()

    def one_pair(slots):
        xs, bands, notes = [], [], []
        for group, rank in slots:
            got = src_ref[group * cap + rank]
            valid = got >= 0
            b = jnp.maximum(got, 0)
            xs.append(x_ref[b].astype(F32))
            own = (block_lane == b) & valid
            column = jnp.sum(jnp.where(own, coefs, 0.0), axis=1, keepdims=True)
            diff = diff_ref[...] - off_ref[b]
            band = jnp.zeros(diff.shape, F32)
            for t in range(6):
                band = jnp.where(diff == t, column[t : t + 1, :], band)
            bands.append(band)
            slot = jnp.where(valid, dest_ref[b] % blocks, -1).astype(F32)
            weight = jnp.sum(jnp.where(own, wgt_ref[...], 0.0), axis=1, keepdims=True)
            note = jnp.where(lane == 0, slot, 0.0)
            for i, part in enumerate(three(jnp.broadcast_to(weight, (rows, LANE)))):
                note = jnp.where(lane == i + 1, part, note)
            notes.append(note + fit_note if rank == 0 else note)
        x16 = jnp.concatenate(xs, axis=0).astype(BF)
        padded = jnp.concatenate([zero, x16, zero], axis=1)
        windows = jnp.concatenate(
            [padded[:, LANE * t : LANE * (t + 2)] for t in range(tiles + 1)], axis=0
        )
        band = jnp.concatenate(bands, axis=1).astype(BF)
        band = jnp.concatenate([jnp.zeros((ROW0, 2 * LANE), BF), band], axis=0)
        made = dot(windows, band)

        def piece(i):
            at = made[2 * rows * i : 2 * rows * (i + 1)]
            return at[:rows, :LANE], at[rows:, LANE:]

        for t in range(tiles):
            top, bottom = piece(t)
            if t == 0:
                last = piece(tiles)
                top = jnp.where(lane < SHIFT, last[0], top)
                bottom = jnp.where(lane < SHIFT, last[1], bottom)
            put(slots, t, top, bottom)
        put(slots, tiles, notes[0], notes[1])

    def put(slots, t, top, bottom):
        cols = slice(LANE * t, LANE * (t + 1))
        (group0, rank0), (group1, rank1) = slots
        group0, group1 = order.index(group0), order.index(group1)
        if group0 == group1:
            made_ref[group0, rows * rank0 : rows * (rank0 + 2), cols] = jnp.concatenate(
                [top, bottom], axis=0
            ).astype(BF)
        else:
            made_ref[group0, rows * rank0 : rows * (rank0 + 1), cols] = top.astype(BF)
            made_ref[group1, rows * rank1 : rows * (rank1 + 1), cols] = bottom.astype(BF)

    sends = [pltpu.make_async_copy(made_ref.at[i], outs[i], sems.at[6 + i]) for i in range(len(order))]
    for at in range(0, len(order), 2):
        two = order[at : at + 2]
        for group in two:
            for rank in range(0, cap - 1, 2):
                one_pair([(group, rank), (group, rank + 1)])
        if cap % 2:
            one_pair([(two[0], cap - 1), (two[1], cap - 1)])
        for i in range(2):
            sends[at + i].start()
    for send in sends:
        send.wait()


def resample(exposure, dest, offset, shift, weight, fit, peers, cap, order):
    rows_dev, width = exposure.shape
    blocks = dest.shape[0]
    rows = rows_dev // blocks
    hbm = pl.BlockSpec(memory_space=pl.ANY)
    return pl.pallas_call(
        functools.partial(resample_kernel, cap, peers, order, len(fit)),
        in_specs=[hbm] * (5 + len(fit)),
        out_specs=[hbm] * len(order),
        out_shape=[jax.ShapeDtypeStruct((cap * rows, width + LANE), BF)] * len(order),
        scratch_shapes=[
            pltpu.SMEM((blocks,), jnp.int32),
            pltpu.SMEM((blocks,), jnp.int32),
            pltpu.SMEM((peers * cap,), jnp.int32),
            pltpu.SMEM((peers,), jnp.int32),
            pltpu.VMEM((1, blocks), F32),
            pltpu.VMEM((1, blocks), F32),
            pltpu.VMEM((blocks, rows, width), BF),
            pltpu.VMEM((len(order), cap * rows, width + LANE), BF),
            pltpu.VMEM((2 * LANE - ROW0, LANE), jnp.int32),
            pltpu.VMEM((1, LANE), F32),
            pltpu.SemaphoreType.DMA((6 + len(order),)),
        ],
        compiler_params=pltpu.CompilerParams(vmem_limit_bytes=LATE_VMEM if fit else EARLY_VMEM),
        name="resample",
    )(dest, offset, shift.reshape(1, blocks), weight.reshape(1, blocks), exposure.reshape(blocks, rows, width), *fit)


def gauss_band(shape, rows_axis, width, total):
    u = lax.broadcasted_iota(jnp.int32, shape, 1 - rows_axis)
    u = u - lax.broadcasted_iota(jnp.int32, shape, rows_axis) - 1
    at = (u - HALF).astype(F32)
    value = jnp.exp(-(at * at) / (2.0 * width * width)) / total
    return jnp.where((u >= 0) & (u < TAPS), value, 0.0).astype(BF)


def tables_kernel(width_ref, band_ref, inner_ref, edge_ref):
    inner, rows_dev = inner_ref.shape[1:]
    edge_ref[...] = jnp.zeros(edge_ref.shape, BF)
    for k in range(BASES):
        width = jnp.full((8, LANE), width_ref[k], F32)[:1, :1]
        tap = lax.broadcasted_iota(jnp.int32, (1, LANE), 1)
        at = (tap - HALF).astype(F32)
        each = jnp.where(tap < TAPS, jnp.exp(-(at * at) / (2.0 * width * width)), 0.0)
        total = jnp.sum(each, axis=1, keepdims=True)
        band_ref[:, LANE * k : LANE * (k + 1)] = gauss_band((2 * LANE, LANE), 1, width, total)
        inner_ref[k] = gauss_band((inner, rows_dev), 0, width, total)
        strip = gauss_band((EDGE, 3 * EDGE), 0, width, total)
        none = jnp.zeros(strip.shape, BF)
        edge_ref[2 * EDGE * k : 2 * EDGE * k + EDGE, :] = jnp.concatenate([strip, none], axis=1)
        edge_ref[2 * EDGE * k + EDGE : 2 * EDGE * (k + 1), :] = jnp.concatenate([none, strip], axis=1)


def tables(basis_width, rows_dev):
    sd = lambda *shape: jax.ShapeDtypeStruct(shape, BF)
    return pl.pallas_call(
        tables_kernel,
        in_specs=[pl.BlockSpec(memory_space=pltpu.SMEM)],
        out_shape=[
            sd(2 * LANE, BASES * LANE),
            sd(BASES, rows_dev - 2 * EDGE, rows_dev),
            sd(2 * EDGE * BASES, 6 * EDGE),
        ],
        compiler_params=pltpu.CompilerParams(vmem_limit_bytes=SMALL_VMEM),
        name="tables",
    )(basis_width)


def split_rows(groups, rows):
    even = groups[0].shape[0] // (2 * rows) * (2 * rows)
    parts = [jnp.concatenate([g[:even] for g in groups], axis=0)]
    if even < groups[0].shape[0]:
        parts.append(jnp.concatenate([g[even:].astype(F32) for g in groups], axis=0).astype(BF))
    return parts


def plan_slots(notes, rows, rows_dev):
    slots = rows_dev // rows
    fit = sum(sum(g[i : i + 1].astype(F32) for i in range(3)) for g in notes[::2])
    places, column, lined = [], None, None
    for part in split_rows(notes, rows):
        count = part.shape[0]
        slot = part[:, :1].astype(F32)
        across = jnp.broadcast_to(slot, (count, LANE)).T[:1].astype(jnp.int32)
        row = lax.broadcasted_iota(jnp.int32, (rows_dev, 1), 0)
        lane = lax.broadcasted_iota(jnp.int32, (1, count), 1)
        match = (across == row // rows) & (lane % rows == row % rows)
        place = jnp.where(match, 1.0, 0.0).astype(BF)
        sums = dot(place, part)
        column = sums if column is None else column + sums
        places.append(place)
        source = lax.broadcasted_iota(jnp.int32, (count, 1), 0)
        index = lax.broadcasted_iota(jnp.int32, (1, slots), 1)
        match = (slot.astype(jnp.int32) == index) & (source % rows == 0)
        sums = lax.dot_general(
            part, jnp.where(match, 1.0, 0.0).astype(BF), (((0,), (0,)), ((), ())),
            preferred_element_type=F32,
        )
        lined = sums if lined is None else lined + sums
    cover = column[:, 1:2] + column[:, 2:3] + column[:, 3:4]
    scale = jnp.broadcast_to(1.0 / jnp.maximum(cover, 1.0), (rows_dev, LANE))
    return places, scale, lined[1:2] + lined[2:3] + lined[3:4], fit


def coadd_kernel(peers, rows, chunk, *refs):
    groups = refs[:peers]
    image_ref, inward_ref, outward_ref, cover_ref, fit_ref = refs[peers:]
    rows_dev, width = image_ref.shape
    odd = lax.axis_index(BOTH) % 2 == 1
    places, scale, cover, fit = plan_slots([g[:, width:] for g in groups], rows, rows_dev)
    cover_ref[...] = cover
    fit_ref[...] = fit
    for at in range(0, width, chunk):
        cols = slice(at, at + chunk)
        value = None
        for part, place in zip(split_rows([g[:, cols] for g in groups], rows), places):
            sums = dot(place, part)
            value = sums if value is None else value + sums
        value = (value * scale[:, :1]).astype(BF)
        image_ref[:, cols] = value
        top, bottom = value[:EDGE], value[rows_dev - EDGE :]
        inward_ref[:, cols] = jnp.where(odd, top, bottom)
        outward_ref[:, cols] = jnp.where(odd, bottom, top)


def coadd(groups, rows_dev, rows):
    peers = len(groups)
    width = groups[0].shape[1] - LANE
    sd = jax.ShapeDtypeStruct
    vmem = pl.BlockSpec(memory_space=pltpu.VMEM)
    return pl.pallas_call(
        functools.partial(coadd_kernel, peers, rows, CHUNK2),
        in_specs=[vmem] * peers,
        out_specs=[vmem] * 5,
        out_shape=[
            sd((rows_dev, width), BF),
            sd((EDGE, width), BF),
            sd((EDGE, width), BF),
            sd((1, rows_dev // rows), F32),
            sd((1, LANE), F32),
        ],
        compiler_params=pltpu.CompilerParams(vmem_limit_bytes=SMALL_VMEM),
        name="coadd",
    )(*groups)


def row_position(base, count, all_rows):
    at = (base + lax.broadcasted_iota(jnp.int32, (count, 1), 0)).astype(F32)
    return 2.0 * at / (all_rows - 1) - 1.0


def col_position(first, count, col_count):
    at = (first + lax.broadcasted_iota(jnp.int32, (1, count), 1)).astype(F32)
    return 2.0 * at / (col_count - 1) - 1.0


def field(fit_ref, k, y, xx):
    c = lambda i: fit_ref[0, FIT0 + NPOLY * k + i]
    return (c(0) + c(2) * y + c(5) * y * y) + (c(1) + c(4) * y) * xx + c(3) * (xx * xx)


def lane_of(value):
    return lax.broadcasted_iota(jnp.int32, (1, value.shape[1]), 1)


def blank(value, keep):
    return jnp.where(keep, value, jnp.zeros_like(value))


def tile_windows(value, tiles):
    return jnp.concatenate([value[:, LANE * t : LANE * (t + 2)] for t in range(tiles)], axis=0)


def inner_rows(image, first, start, fit_ref, band_ref, inner_ref, all_rows, col_count):
    rows_dev, width = image.shape
    inner = rows_dev - 2 * EDGE
    tiles = width // LANE - 1
    smooth = dot(tile_windows(image, tiles), band_ref[...]).astype(BF)
    y = row_position(start + EDGE, inner, all_rows)
    xx = col_position(first, LANE * tiles, col_count)
    total = None
    for k in range(BASES):
        part = jnp.concatenate(
            [smooth[rows_dev * t : rows_dev * (t + 1), LANE * k : LANE * (k + 1)] for t in range(tiles)],
            axis=1,
        )
        term = field(fit_ref, k, y, xx) * dot(inner_ref[k], part)
        total = term if total is None else total + term
    return total.astype(BF)


def inner_kernel(
    all_rows, chunk, start_ref, fit_ref, image_ref, band_ref, inner_ref, out_ref, made_ref, sems
):
    rows_dev, col_count = image_ref.shape
    inner = rows_dev - 2 * EDGE
    sends = []
    for at in range(0, col_count, chunk):
        x = image_ref[:, at : at + chunk]
        head, tail = x[:, :LANE], image_ref[:, (at + chunk) % col_count :][:, :LANE]
        if at == 0:
            head = blank(head, lane_of(head) >= SHIFT)
        if at + chunk == col_count:
            tail = blank(tail, lane_of(tail) < SHIFT)
        image = jnp.concatenate([head, x[:, LANE:], tail], axis=1)
        value = inner_rows(
            image, at, start_ref[0], fit_ref, band_ref, inner_ref, all_rows, col_count
        )
        slot = len(sends) % 2
        if len(sends) >= 2:
            sends[-2].wait()
        made_ref[slot] = value
        send = pltpu.make_async_copy(
            made_ref.at[slot], out_ref.at[pl.ds(EDGE, inner), pl.ds(at, chunk)], sems.at[slot]
        )
        send.start()
        sends.append(send)
    for send in sends[-2:]:
        send.wait()


def whole_of(v):
    return pl.BlockSpec(v.shape, lambda i: (0,) * v.ndim)


def match_inner(image, start, fit, band, inner, all_rows):
    rows_dev, col_count = image.shape
    chunk = CHUNK3
    smem = pl.BlockSpec(memory_space=pltpu.SMEM)
    vmem = pl.BlockSpec(memory_space=pltpu.VMEM)
    return pl.pallas_call(
        functools.partial(inner_kernel, all_rows, chunk),
        in_specs=[smem, smem, vmem, vmem, vmem],
        out_specs=pl.BlockSpec(memory_space=pl.ANY),
        out_shape=jax.ShapeDtypeStruct((rows_dev, col_count), BF),
        scratch_shapes=[
            pltpu.VMEM((2, rows_dev - 2 * EDGE, chunk), BF),
            pltpu.SemaphoreType.DMA((2,)),
        ],
        compiler_params=pltpu.CompilerParams(vmem_limit_bytes=MATCH_VMEM),
        name="match_inner",
    )(start, fit, image, band, inner)


def edge_kernel(
    all_rows, rows_dev, start_ref, fit_ref, inward_ref, image_ref, outward_ref, band_ref,
    edge_ref, old_ref, out_ref, made_ref, sems,
):
    col_count = made_ref.shape[1]
    tiles = col_count // LANE
    odd = lax.axis_index(BOTH) % 2 == 1
    inward, outward = inward_ref[...], outward_ref[...]
    above, below = jnp.where(odd, inward, outward), jnp.where(odd, outward, inward)
    top, bottom = image_ref[: 2 * EDGE], image_ref[rows_dev - 2 * EDGE :]
    x = jnp.concatenate([above, top, bottom, below], axis=0)
    rowconv = dot(edge_ref[...], x).astype(BF)
    head = rowconv[:, :LANE]
    rowconv = jnp.concatenate(
        [blank(head, lane_of(head) >= SHIFT), rowconv[:, LANE:], blank(head, lane_of(head) < SHIFT)],
        axis=1,
    )
    y = jnp.concatenate(
        [row_position(start_ref[0] + at, EDGE, all_rows) for at in (0, rows_dev - EDGE)], axis=0
    )
    both = 2 * EDGE
    parts = [
        dot(tile_windows(rowconv[both * k : both * (k + 1)], tiles), band_ref[:, LANE * k : LANE * (k + 1)])
        for k in range(BASES)
    ]
    for t in range(tiles):
        xx = col_position(LANE * t, LANE, col_count)
        total = None
        for k in range(BASES):
            term = field(fit_ref, k, y, xx) * parts[k][both * t : both * (t + 1)]
            total = term if total is None else total + term
        made_ref[:, LANE * t : LANE * (t + 1)] = total.astype(BF)
    copies = [
        pltpu.make_async_copy(
            made_ref.at[pl.ds(EDGE * i, EDGE)], out_ref.at[pl.ds(at, EDGE)], sems.at[i]
        )
        for i, at in enumerate((0, rows_dev - EDGE))
    ]
    for copy in copies:
        copy.start()
    for copy in copies:
        copy.wait()


def match_edges(matched, image, halos, start, fit, band, edge, all_rows):
    rows_dev, col_count = matched.shape
    smem = pl.BlockSpec(memory_space=pltpu.SMEM)
    vmem = pl.BlockSpec(memory_space=pltpu.VMEM)
    hbm = pl.BlockSpec(memory_space=pl.ANY)
    return pl.pallas_call(
        functools.partial(edge_kernel, all_rows, rows_dev),
        in_specs=[smem, smem] + [vmem] * 5 + [hbm],
        out_specs=hbm,
        out_shape=jax.ShapeDtypeStruct(matched.shape, BF),
        scratch_shapes=[pltpu.VMEM((2 * EDGE, col_count), BF), pltpu.SemaphoreType.DMA((2,))],
        input_output_aliases={7: 0},
        compiler_params=pltpu.CompilerParams(vmem_limit_bytes=SMALL_VMEM),
        name="match_edges",
    )(start, fit, halos[0], image, halos[1], band, edge, matched)


def shards(
    exposure, block_dest, band_offset, col_shift, block_weight, basis_width, kernel_fit, fit_owner
):
    rows_dev, _ = exposure.shape
    blocks = block_dest.shape[0]
    peers = lax.axis_size("patch")
    dets = lax.axis_size("det")
    devices = lax.axis_size(BOTH)
    cap = blocks // peers + 1
    me = lax.axis_index(BOTH)
    all_rows = rows_dev * devices
    start = jnp.full((1,), me * rows_dev, jnp.int32)
    send = lambda group, s: lax.ppermute(
        group, "patch", [(i, i ^ s) for i in range(peers)]
    )
    order = sorted(range(peers), key=lambda s: (s % 2 == 0, -s))
    early_order = order[:2]
    late_order = sorted(order[2:], key=lambda s: -s)
    partner_fit = lax.ppermute(kernel_fit, "patch", [(i, i ^ 1) for i in range(peers)])
    source = (exposure, block_dest, band_offset, col_shift, block_weight)
    early = resample(*source, [], peers, cap, early_order)
    groups = {s: send(group, s) for s, group in zip(early_order, early)}
    source, early, fit, partner_fit = lax.optimization_barrier(
        (source, early, kernel_fit, partner_fit)
    )
    owner = fit_owner[0]
    partner = me ^ 1
    fit = jnp.where(me == owner, fit, 0.0) + jnp.where(partner == owner, partner_fit, 0.0)
    fit = fit.reshape(1, BASES * NPOLY)
    span = 1
    while span < dets:
        fit = fit + lax.ppermute(fit, "det", [(i, i ^ span) for i in range(dets)])
        span *= 2
    fit = jnp.pad(fit, ((0, 0), (0, LANE - BASES * NPOLY)))
    fit = jnp.roll(fit, FIT0, axis=1)
    late = resample(*source, [fit], peers, cap, late_order)
    for s, group in zip(late_order, late):
        groups[s] = send(group, s) if s else group
    late, basis_width = lax.optimization_barrier((late, basis_width))
    band, inner, edge = tables(basis_width, rows_dev)
    groups = [groups[s] for s in range(peers)]
    groups, band, inner, edge = lax.optimization_barrier((groups, band, inner, edge))
    image, inward, outward, cover, fit = coadd(groups, rows_dev, rows_dev // blocks)
    even = [(i, i ^ 1) for i in range(devices)]
    odd = [(i, j) for j in range(2, devices, 2) for i, j in ((j, j - 1), (j - 1, j))]
    halos = (lax.ppermute(inward, BOTH, even), lax.ppermute(outward, BOTH, odd))
    matched = match_inner(image, start, fit, band, inner, all_rows)
    matched = match_edges(matched, image, halos, start, fit, band, edge, all_rows)
    return matched, cover.reshape(blocks)


def solution(mesh):
    in_specs = (
        P(BOTH, None),
        P(BOTH),
        P(BOTH),
        P(BOTH),
        P(BOTH),
        P(),
        P(BOTH, None, None),
        P(),
    )
    out_specs = (P(BOTH, None), P(BOTH))
    return jax.shard_map(shards, mesh=mesh, in_specs=in_specs, out_specs=out_specs, check_vma=False)
```

```python
import functools
import math

import jax
import jax.numpy as jnp
from jax import lax
from jax.experimental import pallas as pl
from jax.experimental.pallas import tpu as pltpu
from jax.sharding import PartitionSpec as P

TAPS = 31
HALF = 15
BASES = 3
NPOLY = 6
LANE = 128
SHIFT = 16
EDGE = 16
BOTH = ("det", "patch")
BF = jnp.bfloat16
F32 = jnp.float32
MIB = 1 << 20
EARLY_VMEM, LATE_VMEM = 62 * MIB, 32 * MIB
SMALL_VMEM, MATCH_VMEM = 24 * MIB, 32 * MIB
ROW0 = 96
FIT0 = 32
CHUNK2 = 2048
CHUNK3 = 2048


def dot(a, b):
    return jnp.dot(a, b, preferred_element_type=F32)


def lanczos(position):
    def sinc(v):
        at = jnp.where(v == 0.0, 1.0, math.pi * v)
        return jnp.where(v == 0.0, 1.0, jnp.sin(at) / at)

    return sinc(position) * sinc(position / 3.0)


def resample_kernel(cap, peers, order, with_fit, *refs):
    dest_hbm, off_hbm, shift_hbm, wgt_hbm, x_hbm = refs[:5]
    outs = refs[5 + with_fit : -11]
    (
        dest_ref, off_ref, src_ref, count_ref, shift_ref, wgt_ref, x_ref, made_ref, diff_ref,
        fit_ref, sems,
    ) = refs[-11:]
    blocks, rows, width = dest_ref.shape[0], x_ref.shape[0] // dest_ref.shape[0], x_ref.shape[1]
    tiles = width // LANE
    me = lax.axis_index("patch")
    smalls = [(dest_hbm, dest_ref), (off_hbm, off_ref), (shift_hbm, shift_ref), (wgt_hbm, wgt_ref)]
    if with_fit:
        smalls.append((refs[5], fit_ref))
    copies = [
        pltpu.make_async_copy(source, target, sems.at[i])
        for i, (source, target) in enumerate([(x_hbm, x_ref)] + smalls)
    ]
    for copy in copies:
        copy.start()
    diff_ref[...] = (
        lax.broadcasted_iota(jnp.int32, diff_ref.shape, 0)
        - lax.broadcasted_iota(jnp.int32, diff_ref.shape, 1)
        + (ROW0 - (LANE - SHIFT - 2))
    )
    for p in range(peers):
        count_ref[p] = 0
    for q in range(peers * cap):
        src_ref[q] = -1
    for copy in copies[1:]:
        copy.wait()
    for b in range(blocks):
        group = (dest_ref[b] // blocks % peers) ^ me
        rank = count_ref[group]
        src_ref[group * cap + rank] = b
        count_ref[group] = rank + 1
    tap = lax.broadcasted_iota(jnp.int32, (8, blocks), 0).astype(F32) - 2.0
    coefs = lanczos(tap - shift_ref[...]) * wgt_ref[...]
    lane = lax.broadcasted_iota(jnp.int32, (rows, LANE), 1)
    block_lane = lax.broadcasted_iota(jnp.int32, (8, blocks), 1)
    zero = jnp.zeros((2 * rows, LANE), BF)

    def three(value):
        high = value.astype(BF).astype(F32)
        mid = (value - high).astype(BF).astype(F32)
        return high, mid, value - high - mid

    fit_note = jnp.zeros((rows, LANE), F32)
    line = lax.broadcasted_iota(jnp.int32, (rows, LANE), 0)
    if with_fit:
        for i, part in enumerate(three(jnp.broadcast_to(fit_ref[...], (rows, LANE)))):
            fit_note = jnp.where(line == i, part, fit_note)
    copies[0].wait()

    def one_pair(slots):
        xs, bands, notes = [], [], []
        for group, rank in slots:
            got = src_ref[group * cap + rank]
            valid = got >= 0
            b = jnp.maximum(got, 0)
            two = x_ref[pl.ds(pl.multiple_of(b // 2 * 2 * rows, 2 * rows), 2 * rows), :].astype(F32)
            xs.append(jnp.where(b % 2 == 1, two[rows:], two[:rows]))
            own = (block_lane == b) & valid
            column = jnp.sum(jnp.where(own, coefs, 0.0), axis=1, keepdims=True)
            diff = diff_ref[...] - off_ref[b]
            band = jnp.zeros(diff.shape, F32)
            for t in range(6):
                band = jnp.where(diff == t, column[t : t + 1, :], band)
            bands.append(band)
            slot = jnp.where(valid, dest_ref[b] % blocks, -1).astype(F32)
            weight = jnp.sum(jnp.where(own, wgt_ref[...], 0.0), axis=1, keepdims=True)
            note = jnp.where(lane == 0, slot, 0.0)
            for i, part in enumerate(three(jnp.broadcast_to(weight, (rows, LANE)))):
                note = jnp.where(lane == i + 1, part, note)
            notes.append(note + fit_note if rank == 0 else note)
        x16 = jnp.concatenate(xs, axis=0).astype(BF)
        padded = jnp.concatenate([zero, x16, zero], axis=1)
        windows = jnp.concatenate(
            [padded[:, LANE * t : LANE * (t + 2)] for t in range(tiles + 1)], axis=0
        )
        band = jnp.concatenate(bands, axis=1).astype(BF)
        band = jnp.concatenate([jnp.zeros((ROW0, 2 * LANE), BF), band], axis=0)
        made = dot(windows, band)

        def piece(i):
            at = made[2 * rows * i : 2 * rows * (i + 1)]
            return at[:rows, :LANE], at[rows:, LANE:]

        tops, bottoms = [list(half) for half in zip(*(piece(t) for t in range(tiles)))]
        last = piece(tiles)
        tops[0] = jnp.where(lane < SHIFT, last[0], tops[0])
        bottoms[0] = jnp.where(lane < SHIFT, last[1], bottoms[0])
        tops.append(notes[0])
        bottoms.append(notes[1])
        (group0, rank0), (group1, rank1) = slots
        if group0 == group1:
            for t in range(tiles + 1):
                put(group0, rank0 // 2 * (tiles + 1) + t, tops[t], bottoms[t])
        else:
            half = tiles // 2 + 1
            for group, pieces in ((group0, tops), (group1, bottoms)):
                pieces = pieces + [jnp.zeros((rows, LANE), F32)] * (2 * half - len(pieces))
                for t in range(half):
                    put(group, cap // 2 * (tiles + 1) + t, pieces[t], pieces[t + half])

    def put(group, tile, top, bottom):
        made_ref[order.index(group), :, LANE * tile : LANE * (tile + 1)] = jnp.concatenate(
            [top, bottom], axis=0
        ).astype(BF)

    sends = [pltpu.make_async_copy(made_ref.at[i], outs[i], sems.at[6 + i]) for i in range(len(order))]
    for at in range(0, len(order), 2):
        two = order[at : at + 2]
        for group in two:
            for rank in range(0, cap - 1, 2):
                one_pair([(group, rank), (group, rank + 1)])
        if cap % 2:
            one_pair([(two[0], cap - 1), (two[1], cap - 1)])
        for i in range(2):
            sends[at + i].start()
    for send in sends:
        send.wait()


def message_shape(cap, rows, width):
    tiles = width // LANE
    return 2 * rows, LANE * (cap // 2 * (tiles + 1) + cap % 2 * (tiles // 2 + 1))


def resample(exposure, dest, offset, shift, weight, fit, peers, cap, order):
    rows_dev, width = exposure.shape
    blocks = dest.shape[0]
    rows = rows_dev // blocks
    hbm = pl.BlockSpec(memory_space=pl.ANY)
    return pl.pallas_call(
        functools.partial(resample_kernel, cap, peers, order, len(fit)),
        in_specs=[hbm] * (5 + len(fit)),
        out_specs=[hbm] * len(order),
        out_shape=[jax.ShapeDtypeStruct(message_shape(cap, rows, width), BF)] * len(order),
        scratch_shapes=[
            pltpu.SMEM((blocks,), jnp.int32),
            pltpu.SMEM((blocks,), jnp.int32),
            pltpu.SMEM((peers * cap,), jnp.int32),
            pltpu.SMEM((peers,), jnp.int32),
            pltpu.VMEM((1, blocks), F32),
            pltpu.VMEM((1, blocks), F32),
            pltpu.VMEM((rows_dev, width), BF),
            pltpu.VMEM((len(order),) + message_shape(cap, rows, width), BF),
            pltpu.VMEM((2 * LANE - ROW0, LANE), jnp.int32),
            pltpu.VMEM((1, LANE), F32),
            pltpu.SemaphoreType.DMA((6 + len(order),)),
        ],
        compiler_params=pltpu.CompilerParams(vmem_limit_bytes=LATE_VMEM if fit else EARLY_VMEM),
        name="resample",
    )(dest, offset, shift.reshape(1, blocks), weight.reshape(1, blocks), exposure, *fit)


def gauss_band(shape, rows_axis, width, total):
    u = lax.broadcasted_iota(jnp.int32, shape, 1 - rows_axis)
    u = u - lax.broadcasted_iota(jnp.int32, shape, rows_axis) - 1
    at = (u - HALF).astype(F32)
    value = jnp.exp(-(at * at) / (2.0 * width * width)) / total
    return jnp.where((u >= 0) & (u < TAPS), value, 0.0).astype(BF)


def tables_kernel(width_ref, band_ref, inner_ref, edge_ref):
    inner, rows_dev = inner_ref.shape[1:]
    edge_ref[...] = jnp.zeros(edge_ref.shape, BF)
    for k in range(BASES):
        width = jnp.full((8, LANE), width_ref[k], F32)[:1, :1]
        tap = lax.broadcasted_iota(jnp.int32, (1, LANE), 1)
        at = (tap - HALF).astype(F32)
        each = jnp.where(tap < TAPS, jnp.exp(-(at * at) / (2.0 * width * width)), 0.0)
        total = jnp.sum(each, axis=1, keepdims=True)
        band_ref[:, LANE * k : LANE * (k + 1)] = gauss_band((2 * LANE, LANE), 1, width, total)
        inner_ref[k] = gauss_band((inner, rows_dev), 0, width, total)
        strip = gauss_band((EDGE, 3 * EDGE), 0, width, total)
        none = jnp.zeros(strip.shape, BF)
        edge_ref[2 * EDGE * k : 2 * EDGE * k + EDGE, :] = jnp.concatenate([strip, none], axis=1)
        edge_ref[2 * EDGE * k + EDGE : 2 * EDGE * (k + 1), :] = jnp.concatenate([none, strip], axis=1)


def tables(basis_width, rows_dev):
    sd = lambda *shape: jax.ShapeDtypeStruct(shape, BF)
    return pl.pallas_call(
        tables_kernel,
        in_specs=[pl.BlockSpec(memory_space=pltpu.SMEM)],
        out_shape=[
            sd(2 * LANE, BASES * LANE),
            sd(BASES, rows_dev - 2 * EDGE, rows_dev),
            sd(2 * EDGE * BASES, 6 * EDGE),
        ],
        compiler_params=pltpu.CompilerParams(vmem_limit_bytes=SMALL_VMEM),
        name="tables",
    )(basis_width)


def split_rows(groups, cap, tiles, first, count):
    parts = []
    at = [LANE * (pair * (tiles + 1) + first) for pair in range(cap // 2)]
    if at:
        pairs = [g[:, a : a + LANE * count] for g in groups for a in at]
        parts.append(jnp.concatenate(pairs, axis=0))
    if cap % 2:
        half, base = tiles // 2 + 1, cap // 2 * (tiles + 1)
        upper, lower = max(0, min(half, first + count) - first), max(0, first + count - max(first, half))
        alone = []
        for g in groups:
            rows = g.shape[0] // 2
            pieces = []
            if upper:
                a = LANE * (base + first)
                pieces.append(g[:, a : a + LANE * upper].astype(F32)[:rows])
            if lower:
                a = LANE * (base + max(first, half) - half)
                pieces.append(g[:, a : a + LANE * lower].astype(F32)[rows:])
            alone.append(jnp.concatenate(pieces, axis=1))
        parts.append(jnp.concatenate(alone, axis=0).astype(BF))
    return parts


def plan_slots(notes, rows, rows_dev, cap, peers):
    slots = rows_dev // rows
    size = cap // 2 * 2 * rows
    fit = sum(
        notes[0][size * g + i : size * g + i + 1].astype(F32) for g in range(0, peers, 2) for i in range(3)
    )
    places, column, lined = [], None, None
    for part in notes:
        count = part.shape[0]
        slot = part[:, :1].astype(F32)
        across = jnp.broadcast_to(slot, (count, LANE)).T[:1].astype(jnp.int32)
        row = lax.broadcasted_iota(jnp.int32, (rows_dev, 1), 0)
        lane = lax.broadcasted_iota(jnp.int32, (1, count), 1)
        match = (across == row // rows) & (lane % rows == row % rows)
        place = jnp.where(match, 1.0, 0.0).astype(BF)
        sums = dot(place, part)
        column = sums if column is None else column + sums
        places.append(place)
        source = lax.broadcasted_iota(jnp.int32, (count, 1), 0)
        index = lax.broadcasted_iota(jnp.int32, (1, slots), 1)
        match = (slot.astype(jnp.int32) == index) & (source % rows == 0)
        sums = lax.dot_general(
            part, jnp.where(match, 1.0, 0.0).astype(BF), (((0,), (0,)), ((), ())),
            preferred_element_type=F32,
        )
        lined = sums if lined is None else lined + sums
    cover = column[:, 1:2] + column[:, 2:3] + column[:, 3:4]
    scale = jnp.broadcast_to(1.0 / jnp.maximum(cover, 1.0), (rows_dev, LANE))
    return places, scale, lined[1:2] + lined[2:3] + lined[3:4], fit


def coadd_kernel(peers, cap, rows, chunk, *refs):
    groups = refs[:peers]
    image_ref, inward_ref, outward_ref, cover_ref, fit_ref = refs[peers:]
    rows_dev, width = image_ref.shape
    tiles = width // LANE
    odd = lax.axis_index(BOTH) % 2 == 1
    notes = split_rows(groups, cap, tiles, tiles, 1)
    places, scale, cover, fit = plan_slots(notes, rows, rows_dev, cap, peers)
    cover_ref[...] = cover
    fit_ref[...] = fit
    for at in range(0, width, chunk):
        cols = slice(at, at + chunk)
        value = None
        for part, place in zip(split_rows(groups, cap, tiles, at // LANE, chunk // LANE), places):
            sums = dot(place, part)
            value = sums if value is None else value + sums
        value = (value * scale[:, :1]).astype(BF)
        image_ref[:, cols] = value
        top, bottom = value[:EDGE], value[rows_dev - EDGE :]
        inward_ref[:, cols] = jnp.where(odd, top, bottom)
        outward_ref[:, cols] = jnp.where(odd, bottom, top)


def coadd(groups, cap, rows_dev, rows, width):
    peers = len(groups)
    sd = jax.ShapeDtypeStruct
    vmem = pl.BlockSpec(memory_space=pltpu.VMEM)
    return pl.pallas_call(
        functools.partial(coadd_kernel, peers, cap, rows, CHUNK2),
        in_specs=[vmem] * peers,
        out_specs=[vmem] * 5,
        out_shape=[
            sd((rows_dev, width), BF),
            sd((EDGE, width), BF),
            sd((EDGE, width), BF),
            sd((1, rows_dev // rows), F32),
            sd((1, LANE), F32),
        ],
        compiler_params=pltpu.CompilerParams(vmem_limit_bytes=SMALL_VMEM),
        name="coadd",
    )(*groups)


def row_position(base, count, all_rows):
    at = (base + lax.broadcasted_iota(jnp.int32, (count, 1), 0)).astype(F32)
    return 2.0 * at / (all_rows - 1) - 1.0


def col_position(first, count, col_count):
    at = (first + lax.broadcasted_iota(jnp.int32, (1, count), 1)).astype(F32)
    return 2.0 * at / (col_count - 1) - 1.0


def field(fit_ref, k, y, xx):
    c = lambda i: fit_ref[0, FIT0 + NPOLY * k + i]
    return (c(0) + c(2) * y + c(5) * y * y) + (c(1) + c(4) * y) * xx + c(3) * (xx * xx)


def lane_of(value):
    return lax.broadcasted_iota(jnp.int32, (1, value.shape[1]), 1)


def blank(value, keep):
    return jnp.where(keep, value, jnp.zeros_like(value))


def tile_windows(value, tiles):
    return jnp.concatenate([value[:, LANE * t : LANE * (t + 2)] for t in range(tiles)], axis=0)


def inner_rows(image, first, start, fit_ref, band_ref, inner_ref, all_rows, col_count):
    rows_dev, width = image.shape
    inner = rows_dev - 2 * EDGE
    tiles = width // LANE - 1
    smooth = dot(tile_windows(image, tiles), band_ref[...]).astype(BF)
    y = row_position(start + EDGE, inner, all_rows)
    xx = col_position(first, LANE * tiles, col_count)
    total = None
    for k in range(BASES):
        part = jnp.concatenate(
            [smooth[rows_dev * t : rows_dev * (t + 1), LANE * k : LANE * (k + 1)] for t in range(tiles)],
            axis=1,
        )
        term = field(fit_ref, k, y, xx) * dot(inner_ref[k], part)
        total = term if total is None else total + term
    return total.astype(BF)


def inner_kernel(
    all_rows, chunk, start_ref, fit_ref, image_ref, band_ref, inner_ref, out_ref, made_ref, sems
):
    rows_dev, col_count = image_ref.shape
    inner = rows_dev - 2 * EDGE
    sends = []
    for at in range(0, col_count, chunk):
        x = image_ref[:, at : at + chunk]
        head, tail = x[:, :LANE], image_ref[:, (at + chunk) % col_count :][:, :LANE]
        if at == 0:
            head = blank(head, lane_of(head) >= SHIFT)
        if at + chunk == col_count:
            tail = blank(tail, lane_of(tail) < SHIFT)
        image = jnp.concatenate([head, x[:, LANE:], tail], axis=1)
        value = inner_rows(
            image, at, start_ref[0], fit_ref, band_ref, inner_ref, all_rows, col_count
        )
        slot = len(sends) % 2
        if len(sends) >= 2:
            sends[-2].wait()
        made_ref[slot] = value
        send = pltpu.make_async_copy(
            made_ref.at[slot], out_ref.at[pl.ds(EDGE, inner), pl.ds(at, chunk)], sems.at[slot]
        )
        send.start()
        sends.append(send)
    for send in sends[-2:]:
        send.wait()


def whole_of(v):
    return pl.BlockSpec(v.shape, lambda i: (0,) * v.ndim)


def match_inner(image, start, fit, band, inner, all_rows):
    rows_dev, col_count = image.shape
    chunk = CHUNK3
    smem = pl.BlockSpec(memory_space=pltpu.SMEM)
    vmem = pl.BlockSpec(memory_space=pltpu.VMEM)
    return pl.pallas_call(
        functools.partial(inner_kernel, all_rows, chunk),
        in_specs=[smem, smem, vmem, vmem, vmem],
        out_specs=pl.BlockSpec(memory_space=pl.ANY),
        out_shape=jax.ShapeDtypeStruct((rows_dev, col_count), BF),
        scratch_shapes=[
            pltpu.VMEM((2, rows_dev - 2 * EDGE, chunk), BF),
            pltpu.SemaphoreType.DMA((2,)),
        ],
        compiler_params=pltpu.CompilerParams(vmem_limit_bytes=MATCH_VMEM),
        name="match_inner",
    )(start, fit, image, band, inner)


def edge_kernel(
    all_rows, rows_dev, start_ref, fit_ref, inward_ref, image_ref, outward_ref, band_ref,
    edge_ref, old_ref, out_ref, made_ref, sems,
):
    col_count = made_ref.shape[1]
    tiles = col_count // LANE
    odd = lax.axis_index(BOTH) % 2 == 1
    inward, outward = inward_ref[...], outward_ref[...]
    above, below = jnp.where(odd, inward, outward), jnp.where(odd, outward, inward)
    top, bottom = image_ref[: 2 * EDGE], image_ref[rows_dev - 2 * EDGE :]
    x = jnp.concatenate([above, top, bottom, below], axis=0)
    rowconv = dot(edge_ref[...], x).astype(BF)
    head = rowconv[:, :LANE]
    rowconv = jnp.concatenate(
        [blank(head, lane_of(head) >= SHIFT), rowconv[:, LANE:], blank(head, lane_of(head) < SHIFT)],
        axis=1,
    )
    y = jnp.concatenate(
        [row_position(start_ref[0] + at, EDGE, all_rows) for at in (0, rows_dev - EDGE)], axis=0
    )
    both = 2 * EDGE
    parts = [
        dot(tile_windows(rowconv[both * k : both * (k + 1)], tiles), band_ref[:, LANE * k : LANE * (k + 1)])
        for k in range(BASES)
    ]
    for t in range(tiles):
        xx = col_position(LANE * t, LANE, col_count)
        total = None
        for k in range(BASES):
            term = field(fit_ref, k, y, xx) * parts[k][both * t : both * (t + 1)]
            total = term if total is None else total + term
        made_ref[:, LANE * t : LANE * (t + 1)] = total.astype(BF)
    copies = [
        pltpu.make_async_copy(
            made_ref.at[pl.ds(EDGE * i, EDGE)], out_ref.at[pl.ds(at, EDGE)], sems.at[i]
        )
        for i, at in enumerate((0, rows_dev - EDGE))
    ]
    for copy in copies:
        copy.start()
    for copy in copies:
        copy.wait()


def match_edges(matched, image, halos, start, fit, band, edge, all_rows):
    rows_dev, col_count = matched.shape
    smem = pl.BlockSpec(memory_space=pltpu.SMEM)
    vmem = pl.BlockSpec(memory_space=pltpu.VMEM)
    hbm = pl.BlockSpec(memory_space=pl.ANY)
    return pl.pallas_call(
        functools.partial(edge_kernel, all_rows, rows_dev),
        in_specs=[smem, smem] + [vmem] * 5 + [hbm],
        out_specs=hbm,
        out_shape=jax.ShapeDtypeStruct(matched.shape, BF),
        scratch_shapes=[pltpu.VMEM((2 * EDGE, col_count), BF), pltpu.SemaphoreType.DMA((2,))],
        input_output_aliases={7: 0},
        compiler_params=pltpu.CompilerParams(vmem_limit_bytes=SMALL_VMEM),
        name="match_edges",
    )(start, fit, halos[0], image, halos[1], band, edge, matched)


def shards(
    exposure, block_dest, band_offset, col_shift, block_weight, basis_width, kernel_fit, fit_owner
):
    rows_dev, col_count = exposure.shape
    blocks = block_dest.shape[0]
    peers = lax.axis_size("patch")
    dets = lax.axis_size("det")
    devices = lax.axis_size(BOTH)
    cap = blocks // peers + 1
    me = lax.axis_index(BOTH)
    all_rows = rows_dev * devices
    start = jnp.full((1,), me * rows_dev, jnp.int32)
    send = lambda group, s: lax.ppermute(
        group, "patch", [(i, i ^ s) for i in range(peers)]
    )
    order = sorted(range(peers), key=lambda s: (s % 2 == 0, -s))
    early_order = order[:2]
    late_order = sorted(order[2:], key=lambda s: -s)
    partner_fit = lax.ppermute(kernel_fit, "patch", [(i, i ^ 1) for i in range(peers)])
    source = (exposure, block_dest, band_offset, col_shift, block_weight)
    early = resample(*source, [], peers, cap, early_order)
    groups = {s: send(group, s) for s, group in zip(early_order, early)}
    source, early, fit, partner_fit = lax.optimization_barrier(
        (source, early, kernel_fit, partner_fit)
    )
    owner = fit_owner[0]
    partner = me ^ 1
    fit = jnp.where(me == owner, fit, 0.0) + jnp.where(partner == owner, partner_fit, 0.0)
    fit = fit.reshape(1, BASES * NPOLY)
    span = 1
    while span < dets:
        fit = fit + lax.ppermute(fit, "det", [(i, i ^ span) for i in range(dets)])
        span *= 2
    fit = jnp.pad(fit, ((0, 0), (0, LANE - BASES * NPOLY)))
    fit = jnp.roll(fit, FIT0, axis=1)
    late = resample(*source, [fit], peers, cap, late_order)
    for s, group in zip(late_order, late):
        groups[s] = send(group, s) if s else group
    late, basis_width = lax.optimization_barrier((late, basis_width))
    band, inner, edge = tables(basis_width, rows_dev)
    groups = [groups[s] for s in range(peers)]
    groups, band, inner, edge = lax.optimization_barrier((groups, band, inner, edge))
    image, inward, outward, cover, fit = coadd(groups, cap, rows_dev, rows_dev // blocks, col_count)
    even = [(i, i ^ 1) for i in range(devices)]
    odd = [(i, j) for j in range(2, devices, 2) for i, j in ((j, j - 1), (j - 1, j))]
    halos = (lax.ppermute(inward, BOTH, even), lax.ppermute(outward, BOTH, odd))
    matched = match_inner(image, start, fit, band, inner, all_rows)
    matched = match_edges(matched, image, halos, start, fit, band, edge, all_rows)
    return matched, cover.reshape(blocks)


def solution(mesh):
    in_specs = (
        P(BOTH, None),
        P(BOTH),
        P(BOTH),
        P(BOTH),
        P(BOTH),
        P(),
        P(BOTH, None, None),
        P(),
    )
    out_specs = (P(BOTH, None), P(BOTH))
    return jax.shard_map(shards, mesh=mesh, in_specs=in_specs, out_specs=out_specs, check_vma=False)
```

```python
import functools
import math

import jax
import jax.numpy as jnp
from jax import lax
from jax.experimental import pallas as pl
from jax.experimental.pallas import tpu as pltpu
from jax.sharding import PartitionSpec as P

TAPS = 31
HALF = 15
BASES = 3
NPOLY = 6
LANE = 128
SHIFT = 16
EDGE = 16
BOTH = ("det", "patch")
BF = jnp.bfloat16
F32 = jnp.float32
MIB = 1 << 20
EARLY_VMEM, LATE_VMEM = 62 * MIB, 32 * MIB
SMALL_VMEM, MATCH_VMEM = 24 * MIB, 32 * MIB
ROW0 = 96
FIT0 = 32
CHUNK2 = 2048
CHUNK3 = 2048


def dot(a, b):
    return jnp.dot(a, b, preferred_element_type=F32)


def lanczos(position):
    def sinc(v):
        at = jnp.where(v == 0.0, 1.0, math.pi * v)
        return jnp.where(v == 0.0, 1.0, jnp.sin(at) / at)

    return sinc(position) * sinc(position / 3.0)


def resample_kernel(cap, peers, order, with_fit, *refs):
    dest_hbm, off_hbm, shift_hbm, wgt_hbm, x_hbm = refs[:5]
    outs = refs[5 + with_fit : -11]
    (
        dest_ref, off_ref, src_ref, count_ref, shift_ref, wgt_ref, x_ref, made_ref, diff_ref,
        fit_ref, sems,
    ) = refs[-11:]
    blocks, rows, width = dest_ref.shape[0], x_ref.shape[0] // dest_ref.shape[0], x_ref.shape[1]
    tiles = width // LANE
    me = lax.axis_index("patch")
    smalls = [(dest_hbm, dest_ref), (off_hbm, off_ref), (shift_hbm, shift_ref), (wgt_hbm, wgt_ref)]
    if with_fit:
        smalls.append((refs[5], fit_ref))
    copies = [
        pltpu.make_async_copy(source, target, sems.at[i])
        for i, (source, target) in enumerate([(x_hbm, x_ref)] + smalls)
    ]
    for copy in copies:
        copy.start()
    diff_ref[...] = (
        lax.broadcasted_iota(jnp.int32, diff_ref.shape, 0)
        - lax.broadcasted_iota(jnp.int32, diff_ref.shape, 1)
        + (ROW0 - (LANE - SHIFT - 2))
    )
    for p in range(peers):
        count_ref[p] = 0
    for q in range(peers * cap):
        src_ref[q] = -1
    for copy in copies[1:]:
        copy.wait()
    for b in range(blocks):
        group = (dest_ref[b] // blocks % peers) ^ me
        rank = count_ref[group]
        src_ref[group * cap + rank] = b
        count_ref[group] = rank + 1
    tap = lax.broadcasted_iota(jnp.int32, (8, blocks), 0).astype(F32) - 2.0
    coefs = lanczos(tap - shift_ref[...]) * wgt_ref[...]
    lane = lax.broadcasted_iota(jnp.int32, (rows, LANE), 1)
    block_lane = lax.broadcasted_iota(jnp.int32, (8, blocks), 1)
    zero = jnp.zeros((2 * rows, LANE), BF)

    def three(value):
        high = value.astype(BF).astype(F32)
        mid = (value - high).astype(BF).astype(F32)
        return high, mid, value - high - mid

    fit_note = jnp.zeros((rows, LANE), F32)
    line = lax.broadcasted_iota(jnp.int32, (rows, LANE), 0)
    if with_fit:
        for i, part in enumerate(three(jnp.broadcast_to(fit_ref[...], (rows, LANE)))):
            fit_note = jnp.where(line == i, part, fit_note)
    copies[0].wait()

    noted = {}

    def one_pair(slots):
        xs, bands = [], []
        for group, rank in slots:
            got = src_ref[group * cap + rank]
            valid = got >= 0
            b = jnp.maximum(got, 0)
            two = x_ref[pl.ds(pl.multiple_of(b // 2 * 2 * rows, 2 * rows), 2 * rows), :].astype(F32)
            xs.append(jnp.where(b % 2 == 1, two[rows:], two[:rows]))
            own = (block_lane == b) & valid
            column = jnp.sum(jnp.where(own, coefs, 0.0), axis=1, keepdims=True)
            diff = diff_ref[...] - off_ref[b]
            band = jnp.zeros(diff.shape, F32)
            for t in range(6):
                band = jnp.where(diff == t, column[t : t + 1, :], band)
            bands.append(band)
            slot = jnp.where(valid, dest_ref[b] % blocks, -1).astype(F32)
            weight = jnp.sum(jnp.where(own, wgt_ref[...], 0.0), axis=1, keepdims=True)
            note = jnp.where(lane == 0, slot, 0.0)
            for i, part in enumerate(three(jnp.broadcast_to(weight, (rows, LANE)))):
                note = jnp.where(lane == i + 1, part, note)
            noted[group] = jnp.where(line == rank, note, noted.get(group, 0.0))
        x16 = jnp.concatenate(xs, axis=0).astype(BF)
        padded = jnp.concatenate([zero, x16, zero], axis=1)
        windows = jnp.concatenate(
            [padded[:, LANE * t : LANE * (t + 2)] for t in range(tiles + 1)], axis=0
        )
        band = jnp.concatenate(bands, axis=1).astype(BF)
        band = jnp.concatenate([jnp.zeros((ROW0, 2 * LANE), BF), band], axis=0)
        made = dot(windows, band)

        def piece(i):
            at = made[2 * rows * i : 2 * rows * (i + 1)]
            return at[:rows, :LANE], at[rows:, LANE:]

        tops, bottoms = [list(half) for half in zip(*(piece(t) for t in range(tiles)))]
        last = piece(tiles)
        tops[0] = jnp.where(lane < SHIFT, last[0], tops[0])
        bottoms[0] = jnp.where(lane < SHIFT, last[1], bottoms[0])
        (group0, rank0), (group1, rank1) = slots
        if group0 == group1:
            for t in range(tiles):
                put(group0, rank0 // 2 * tiles + t, tops[t], bottoms[t])
        else:
            half = tiles // 2
            for group, pieces in ((group0, tops), (group1, bottoms)):
                for t in range(half):
                    put(group, cap // 2 * tiles + t, pieces[t], pieces[t + half])

    def put(group, tile, top, bottom):
        made_ref[order.index(group), :, LANE * tile : LANE * (tile + 1)] = jnp.concatenate(
            [top, bottom], axis=0
        ).astype(BF)

    sends = [pltpu.make_async_copy(made_ref.at[i], outs[i], sems.at[6 + i]) for i in range(len(order))]
    for at in range(0, len(order), 2):
        two = order[at : at + 2]
        for group in two:
            for rank in range(0, cap - 1, 2):
                one_pair([(group, rank), (group, rank + 1)])
        if cap % 2:
            one_pair([(two[0], cap - 1), (two[1], cap - 1)])
        for group in two:
            put(group, made_ref.shape[2] // LANE - 1, noted[group], fit_note)
        for i in range(2):
            sends[at + i].start()
    for send in sends:
        send.wait()


def message_shape(cap, rows, width):
    tiles = width // LANE
    return 2 * rows, LANE * (cap // 2 * tiles + cap % 2 * (tiles // 2) + 1)


def resample(exposure, dest, offset, shift, weight, fit, peers, cap, order):
    rows_dev, width = exposure.shape
    blocks = dest.shape[0]
    rows = rows_dev // blocks
    hbm = pl.BlockSpec(memory_space=pl.ANY)
    return pl.pallas_call(
        functools.partial(resample_kernel, cap, peers, order, len(fit)),
        in_specs=[hbm] * (5 + len(fit)),
        out_specs=[hbm] * len(order),
        out_shape=[jax.ShapeDtypeStruct(message_shape(cap, rows, width), BF)] * len(order),
        scratch_shapes=[
            pltpu.SMEM((blocks,), jnp.int32),
            pltpu.SMEM((blocks,), jnp.int32),
            pltpu.SMEM((peers * cap,), jnp.int32),
            pltpu.SMEM((peers,), jnp.int32),
            pltpu.VMEM((1, blocks), F32),
            pltpu.VMEM((1, blocks), F32),
            pltpu.VMEM((rows_dev, width), BF),
            pltpu.VMEM((len(order),) + message_shape(cap, rows, width), BF),
            pltpu.VMEM((2 * LANE - ROW0, LANE), jnp.int32),
            pltpu.VMEM((1, LANE), F32),
            pltpu.SemaphoreType.DMA((6 + len(order),)),
        ],
        compiler_params=pltpu.CompilerParams(vmem_limit_bytes=LATE_VMEM if fit else EARLY_VMEM),
        name="resample",
    )(dest, offset, shift.reshape(1, blocks), weight.reshape(1, blocks), exposure, *fit)


def gauss_band(shape, rows_axis, width, total):
    u = lax.broadcasted_iota(jnp.int32, shape, 1 - rows_axis)
    u = u - lax.broadcasted_iota(jnp.int32, shape, rows_axis) - 1
    at = (u - HALF).astype(F32)
    value = jnp.exp(-(at * at) / (2.0 * width * width)) / total
    return jnp.where((u >= 0) & (u < TAPS), value, 0.0).astype(BF)


def tables_kernel(width_ref, band_ref, inner_ref, edge_ref):
    inner, rows_dev = inner_ref.shape[1:]
    edge_ref[...] = jnp.zeros(edge_ref.shape, BF)
    for k in range(BASES):
        width = jnp.full((8, LANE), width_ref[k], F32)[:1, :1]
        tap = lax.broadcasted_iota(jnp.int32, (1, LANE), 1)
        at = (tap - HALF).astype(F32)
        each = jnp.where(tap < TAPS, jnp.exp(-(at * at) / (2.0 * width * width)), 0.0)
        total = jnp.sum(each, axis=1, keepdims=True)
        band_ref[:, LANE * k : LANE * (k + 1)] = gauss_band((2 * LANE, LANE), 1, width, total)
        inner_ref[k] = gauss_band((inner, rows_dev), 0, width, total)
        strip = gauss_band((EDGE, 3 * EDGE), 0, width, total)
        none = jnp.zeros(strip.shape, BF)
        edge_ref[2 * EDGE * k : 2 * EDGE * k + EDGE, :] = jnp.concatenate([strip, none], axis=1)
        edge_ref[2 * EDGE * k + EDGE : 2 * EDGE * (k + 1), :] = jnp.concatenate([none, strip], axis=1)


def tables(basis_width, rows_dev):
    sd = lambda *shape: jax.ShapeDtypeStruct(shape, BF)
    return pl.pallas_call(
        tables_kernel,
        in_specs=[pl.BlockSpec(memory_space=pltpu.SMEM)],
        out_shape=[
            sd(2 * LANE, BASES * LANE),
            sd(BASES, rows_dev - 2 * EDGE, rows_dev),
            sd(2 * EDGE * BASES, 6 * EDGE),
        ],
        compiler_params=pltpu.CompilerParams(vmem_limit_bytes=SMALL_VMEM),
        name="tables",
    )(basis_width)


def split_rows(groups, cap, tiles, first, count):
    parts = []
    at = [LANE * (pair * tiles + first) for pair in range(cap // 2)]
    if at:
        pairs = [g[:, a : a + LANE * count] for g in groups for a in at]
        parts.append(jnp.concatenate(pairs, axis=0))
    if cap % 2:
        half, base = tiles // 2, cap // 2 * tiles
        upper, lower = max(0, min(half, first + count) - first), max(0, first + count - max(first, half))
        alone = []
        for g in groups:
            rows = g.shape[0] // 2
            pieces = []
            if upper:
                a = LANE * (base + first)
                pieces.append(g[:, a : a + LANE * upper].astype(F32)[:rows])
            if lower:
                a = LANE * (base + max(first, half) - half)
                pieces.append(g[:, a : a + LANE * lower].astype(F32)[rows:])
            alone.append(jnp.concatenate(pieces, axis=1))
        parts.append(jnp.concatenate(alone, axis=0).astype(BF))
    return parts


def plan_slots(notes, rows, rows_dev, cap, peers):
    slots, size = rows_dev // rows, 2 * rows
    fit = sum(
        notes[size * g + rows + i : size * g + rows + i + 1].astype(F32)
        for g in range(0, peers, 2)
        for i in range(3)
    )
    spread = lambda at: lax.dot_general(
        notes, jnp.where(at, 1.0, 0.0).astype(BF), (((0,), (0,)), ((), ())), preferred_element_type=F32
    )
    source = lax.broadcasted_iota(jnp.int32, (size * peers, 1), 0)
    row = lax.broadcasted_iota(jnp.int32, (rows_dev, 1), 0)
    even = cap // 2 * 2
    places, cover = [], 0.0
    for first, held in ((0, even), (even, cap - even)):
        if not held:
            continue
        lane = lax.broadcasted_iota(jnp.int32, (1, peers * held * rows), 1)
        block = lane // rows
        told = spread(source == block // held * size + first + block % held)
        match = (told[:1].astype(jnp.int32) == row // rows) & (lane % rows == row % rows)
        places.append(jnp.where(match, 1.0, 0.0).astype(BF))
        weight = told[1:2] + told[2:3] + told[3:4]
        cover = cover + jnp.sum(jnp.where(match, weight, 0.0), axis=1, keepdims=True)
    scale = jnp.broadcast_to(1.0 / jnp.maximum(cover, 1.0), (rows_dev, LANE))
    index = lax.broadcasted_iota(jnp.int32, (1, slots), 1)
    mine = (notes[:, :1].astype(F32).astype(jnp.int32) == index) & (source % size < cap)
    lined = spread(mine)
    return places, scale, lined[1:2] + lined[2:3] + lined[3:4], fit


def coadd_kernel(peers, cap, rows, chunk, *refs):
    groups = refs[:peers]
    image_ref, inward_ref, outward_ref, cover_ref, fit_ref = refs[peers:]
    rows_dev, width = image_ref.shape
    tiles = width // LANE
    odd = lax.axis_index(BOTH) % 2 == 1
    notes = jnp.concatenate([g[:, g.shape[1] - LANE :] for g in groups], axis=0)
    places, scale, cover, fit = plan_slots(notes, rows, rows_dev, cap, peers)
    cover_ref[...] = cover
    fit_ref[...] = fit
    for at in range(0, width, chunk):
        cols = slice(at, at + chunk)
        value = None
        for part, place in zip(split_rows(groups, cap, tiles, at // LANE, chunk // LANE), places):
            sums = dot(place, part)
            value = sums if value is None else value + sums
        value = (value * scale[:, :1]).astype(BF)
        image_ref[:, cols] = value
        top, bottom = value[:EDGE], value[rows_dev - EDGE :]
        inward_ref[:, cols] = jnp.where(odd, top, bottom)
        outward_ref[:, cols] = jnp.where(odd, bottom, top)


def coadd(groups, cap, rows_dev, rows, width):
    peers = len(groups)
    sd = jax.ShapeDtypeStruct
    vmem = pl.BlockSpec(memory_space=pltpu.VMEM)
    return pl.pallas_call(
        functools.partial(coadd_kernel, peers, cap, rows, CHUNK2),
        in_specs=[vmem] * peers,
        out_specs=[vmem] * 5,
        out_shape=[
            sd((rows_dev, width), BF),
            sd((EDGE, width), BF),
            sd((EDGE, width), BF),
            sd((1, rows_dev // rows), F32),
            sd((1, LANE), F32),
        ],
        compiler_params=pltpu.CompilerParams(vmem_limit_bytes=SMALL_VMEM),
        name="coadd",
    )(*groups)


def row_position(base, count, all_rows):
    at = (base + lax.broadcasted_iota(jnp.int32, (count, 1), 0)).astype(F32)
    return 2.0 * at / (all_rows - 1) - 1.0


def col_position(first, count, col_count):
    at = (first + lax.broadcasted_iota(jnp.int32, (1, count), 1)).astype(F32)
    return 2.0 * at / (col_count - 1) - 1.0


def field(fit_ref, k, y, xx):
    c = lambda i: fit_ref[0, FIT0 + NPOLY * k + i]
    return (c(0) + c(2) * y + c(5) * y * y) + (c(1) + c(4) * y) * xx + c(3) * (xx * xx)


def lane_of(value):
    return lax.broadcasted_iota(jnp.int32, (1, value.shape[1]), 1)


def blank(value, keep):
    return jnp.where(keep, value, jnp.zeros_like(value))


def tile_windows(value, tiles):
    return jnp.concatenate([value[:, LANE * t : LANE * (t + 2)] for t in range(tiles)], axis=0)


def inner_rows(image, first, start, fit_ref, band_ref, inner_ref, all_rows, col_count):
    rows_dev, width = image.shape
    inner = rows_dev - 2 * EDGE
    tiles = width // LANE - 1
    smooth = dot(tile_windows(image, tiles), band_ref[...]).astype(BF)
    y = row_position(start + EDGE, inner, all_rows)
    xx = col_position(first, LANE * tiles, col_count)
    total = None
    for k in range(BASES):
        part = jnp.concatenate(
            [smooth[rows_dev * t : rows_dev * (t + 1), LANE * k : LANE * (k + 1)] for t in range(tiles)],
            axis=1,
        )
        term = field(fit_ref, k, y, xx) * dot(inner_ref[k], part)
        total = term if total is None else total + term
    return total.astype(BF)


def inner_kernel(
    all_rows, chunk, start_ref, fit_ref, image_ref, band_ref, inner_ref, out_ref, made_ref, sems
):
    rows_dev, col_count = image_ref.shape
    inner = rows_dev - 2 * EDGE
    sends = []
    for at in range(0, col_count, chunk):
        x = image_ref[:, at : at + chunk]
        head, tail = x[:, :LANE], image_ref[:, (at + chunk) % col_count :][:, :LANE]
        if at == 0:
            head = blank(head, lane_of(head) >= SHIFT)
        if at + chunk == col_count:
            tail = blank(tail, lane_of(tail) < SHIFT)
        image = jnp.concatenate([head, x[:, LANE:], tail], axis=1)
        value = inner_rows(
            image, at, start_ref[0], fit_ref, band_ref, inner_ref, all_rows, col_count
        )
        slot = len(sends) % 2
        if len(sends) >= 2:
            sends[-2].wait()
        made_ref[slot] = value
        send = pltpu.make_async_copy(
            made_ref.at[slot], out_ref.at[pl.ds(EDGE, inner), pl.ds(at, chunk)], sems.at[slot]
        )
        send.start()
        sends.append(send)
    for send in sends[-2:]:
        send.wait()


def whole_of(v):
    return pl.BlockSpec(v.shape, lambda i: (0,) * v.ndim)


def match_inner(image, start, fit, band, inner, all_rows):
    rows_dev, col_count = image.shape
    chunk = CHUNK3
    smem = pl.BlockSpec(memory_space=pltpu.SMEM)
    vmem = pl.BlockSpec(memory_space=pltpu.VMEM)
    return pl.pallas_call(
        functools.partial(inner_kernel, all_rows, chunk),
        in_specs=[smem, smem, vmem, vmem, vmem],
        out_specs=pl.BlockSpec(memory_space=pl.ANY),
        out_shape=jax.ShapeDtypeStruct((rows_dev, col_count), BF),
        scratch_shapes=[
            pltpu.VMEM((2, rows_dev - 2 * EDGE, chunk), BF),
            pltpu.SemaphoreType.DMA((2,)),
        ],
        compiler_params=pltpu.CompilerParams(vmem_limit_bytes=MATCH_VMEM),
        name="match_inner",
    )(start, fit, image, band, inner)


def edge_kernel(
    all_rows, rows_dev, start_ref, fit_ref, inward_ref, image_ref, outward_ref, band_ref,
    edge_ref, old_ref, out_ref, made_ref, sems,
):
    col_count = made_ref.shape[1]
    tiles = col_count // LANE
    odd = lax.axis_index(BOTH) % 2 == 1
    inward, outward = inward_ref[...], outward_ref[...]
    above, below = jnp.where(odd, inward, outward), jnp.where(odd, outward, inward)
    top, bottom = image_ref[: 2 * EDGE], image_ref[rows_dev - 2 * EDGE :]
    x = jnp.concatenate([above, top, bottom, below], axis=0)
    rowconv = dot(edge_ref[...], x).astype(BF)
    head = rowconv[:, :LANE]
    rowconv = jnp.concatenate(
        [blank(head, lane_of(head) >= SHIFT), rowconv[:, LANE:], blank(head, lane_of(head) < SHIFT)],
        axis=1,
    )
    y = jnp.concatenate(
        [row_position(start_ref[0] + at, EDGE, all_rows) for at in (0, rows_dev - EDGE)], axis=0
    )
    both = 2 * EDGE
    parts = [
        dot(tile_windows(rowconv[both * k : both * (k + 1)], tiles), band_ref[:, LANE * k : LANE * (k + 1)])
        for k in range(BASES)
    ]
    for t in range(tiles):
        xx = col_position(LANE * t, LANE, col_count)
        total = None
        for k in range(BASES):
            term = field(fit_ref, k, y, xx) * parts[k][both * t : both * (t + 1)]
            total = term if total is None else total + term
        made_ref[:, LANE * t : LANE * (t + 1)] = total.astype(BF)
    copies = [
        pltpu.make_async_copy(
            made_ref.at[pl.ds(EDGE * i, EDGE)], out_ref.at[pl.ds(at, EDGE)], sems.at[i]
        )
        for i, at in enumerate((0, rows_dev - EDGE))
    ]
    for copy in copies:
        copy.start()
    for copy in copies:
        copy.wait()


def match_edges(matched, image, halos, start, fit, band, edge, all_rows):
    rows_dev, col_count = matched.shape
    smem = pl.BlockSpec(memory_space=pltpu.SMEM)
    vmem = pl.BlockSpec(memory_space=pltpu.VMEM)
    hbm = pl.BlockSpec(memory_space=pl.ANY)
    return pl.pallas_call(
        functools.partial(edge_kernel, all_rows, rows_dev),
        in_specs=[smem, smem] + [vmem] * 5 + [hbm],
        out_specs=hbm,
        out_shape=jax.ShapeDtypeStruct(matched.shape, BF),
        scratch_shapes=[pltpu.VMEM((2 * EDGE, col_count), BF), pltpu.SemaphoreType.DMA((2,))],
        input_output_aliases={7: 0},
        compiler_params=pltpu.CompilerParams(vmem_limit_bytes=SMALL_VMEM),
        name="match_edges",
    )(start, fit, halos[0], image, halos[1], band, edge, matched)


def shards(
    exposure, block_dest, band_offset, col_shift, block_weight, basis_width, kernel_fit, fit_owner
):
    rows_dev, col_count = exposure.shape
    blocks = block_dest.shape[0]
    peers = lax.axis_size("patch")
    dets = lax.axis_size("det")
    devices = lax.axis_size(BOTH)
    cap = blocks // peers + 1
    me = lax.axis_index(BOTH)
    all_rows = rows_dev * devices
    start = jnp.full((1,), me * rows_dev, jnp.int32)
    send = lambda group, s: lax.ppermute(
        group, "patch", [(i, i ^ s) for i in range(peers)]
    )
    order = sorted(range(peers), key=lambda s: (s % 2 == 0, -s))
    early_order = order[:2]
    late_order = sorted(order[2:], key=lambda s: -s)
    partner_fit = lax.ppermute(kernel_fit, "patch", [(i, i ^ 1) for i in range(peers)])
    source = (exposure, block_dest, band_offset, col_shift, block_weight)
    early = resample(*source, [], peers, cap, early_order)
    groups = {s: send(group, s) for s, group in zip(early_order, early)}
    source, early, fit, partner_fit = lax.optimization_barrier(
        (source, early, kernel_fit, partner_fit)
    )
    owner = fit_owner[0]
    partner = me ^ 1
    fit = jnp.where(me == owner, fit, 0.0) + jnp.where(partner == owner, partner_fit, 0.0)
    fit = fit.reshape(1, BASES * NPOLY)
    span = 1
    while span < dets:
        fit = fit + lax.ppermute(fit, "det", [(i, i ^ span) for i in range(dets)])
        span *= 2
    fit = jnp.pad(fit, ((0, 0), (0, LANE - BASES * NPOLY)))
    fit = jnp.roll(fit, FIT0, axis=1)
    late = resample(*source, [fit], peers, cap, late_order)
    for s, group in zip(late_order, late):
        groups[s] = send(group, s) if s else group
    late, basis_width = lax.optimization_barrier((late, basis_width))
    band, inner, edge = tables(basis_width, rows_dev)
    groups = [groups[s] for s in range(peers)]
    groups, band, inner, edge = lax.optimization_barrier((groups, band, inner, edge))
    image, inward, outward, cover, fit = coadd(groups, cap, rows_dev, rows_dev // blocks, col_count)
    even = [(i, i ^ 1) for i in range(devices)]
    odd = [(i, j) for j in range(2, devices, 2) for i, j in ((j, j - 1), (j - 1, j))]
    halos = (lax.ppermute(inward, BOTH, even), lax.ppermute(outward, BOTH, odd))
    matched = match_inner(image, start, fit, band, inner, all_rows)
    matched = match_edges(matched, image, halos, start, fit, band, edge, all_rows)
    return matched, cover.reshape(blocks)


def solution(mesh):
    in_specs = (
        P(BOTH, None),
        P(BOTH),
        P(BOTH),
        P(BOTH),
        P(BOTH),
        P(),
        P(BOTH, None, None),
        P(),
    )
    out_specs = (P(BOTH, None), P(BOTH))
    return jax.shard_map(shards, mesh=mesh, in_specs=in_specs, out_specs=out_specs, check_vma=False)
```

```python
import functools
import math

import jax
import jax.numpy as jnp
from jax import lax
from jax.experimental import pallas as pl
from jax.experimental.pallas import tpu as pltpu
from jax.sharding import PartitionSpec as P

TAPS = 31
HALF = 15
BASES = 3
NPOLY = 6
LANE = 128
SHIFT = 16
EDGE = 16
BOTH = ("det", "patch")
BF = jnp.bfloat16
F32 = jnp.float32
MIB = 1 << 20
EARLY_VMEM, LATE_VMEM = 62 * MIB, 32 * MIB
SMALL_VMEM, MATCH_VMEM = 24 * MIB, 32 * MIB
ROW0 = 96
FIT0 = 32
CHUNK2 = 4096
CHUNK3 = 2048


def dot(a, b):
    return jnp.dot(a, b, preferred_element_type=F32)


def lanczos(position):
    def sinc(v):
        at = jnp.where(v == 0.0, 1.0, math.pi * v)
        return jnp.where(v == 0.0, 1.0, jnp.sin(at) / at)

    return sinc(position) * sinc(position / 3.0)


def resample_kernel(cap, peers, order, with_fit, *refs):
    dest_hbm, off_hbm, shift_hbm, wgt_hbm, x_hbm = refs[:5]
    outs = refs[5 + with_fit : -11]
    (
        dest_ref, off_ref, src_ref, count_ref, shift_ref, wgt_ref, x_ref, made_ref, diff_ref,
        fit_ref, sems,
    ) = refs[-11:]
    blocks, rows, width = dest_ref.shape[0], x_ref.shape[0] // dest_ref.shape[0], x_ref.shape[1]
    tiles = width // LANE
    me = lax.axis_index("patch")
    smalls = [(dest_hbm, dest_ref), (off_hbm, off_ref), (shift_hbm, shift_ref), (wgt_hbm, wgt_ref)]
    if with_fit:
        smalls.append((refs[5], fit_ref))
    copies = [
        pltpu.make_async_copy(source, target, sems.at[i])
        for i, (source, target) in enumerate([(x_hbm, x_ref)] + smalls)
    ]
    for copy in copies:
        copy.start()
    diff_ref[...] = (
        lax.broadcasted_iota(jnp.int32, diff_ref.shape, 0)
        - lax.broadcasted_iota(jnp.int32, diff_ref.shape, 1)
        + (ROW0 - (LANE - SHIFT - 2))
    )
    for p in range(peers):
        count_ref[p] = 0
    for q in range(peers * cap):
        src_ref[q] = -1
    for copy in copies[1:]:
        copy.wait()
    for b in range(blocks):
        group = (dest_ref[b] // blocks % peers) ^ me
        rank = count_ref[group]
        src_ref[group * cap + rank] = b
        count_ref[group] = rank + 1
    tap = lax.broadcasted_iota(jnp.int32, (8, blocks), 0).astype(F32) - 2.0
    coefs = lanczos(tap - shift_ref[...]) * wgt_ref[...]
    lane = lax.broadcasted_iota(jnp.int32, (rows, LANE), 1)
    block_lane = lax.broadcasted_iota(jnp.int32, (8, blocks), 1)
    zero = jnp.zeros((2 * rows, LANE), BF)

    def three(value):
        high = value.astype(BF).astype(F32)
        mid = (value - high).astype(BF).astype(F32)
        return high, mid, value - high - mid

    fit_note = jnp.zeros((rows, LANE), F32)
    line = lax.broadcasted_iota(jnp.int32, (rows, LANE), 0)
    if with_fit:
        for i, part in enumerate(three(jnp.broadcast_to(fit_ref[...], (rows, LANE)))):
            fit_note = jnp.where(line == i, part, fit_note)
    copies[0].wait()

    noted = {}

    def one_pair(slots):
        xs, bands = [], []
        for group, rank in slots:
            got = src_ref[group * cap + rank]
            valid = got >= 0
            b = jnp.maximum(got, 0)
            two = x_ref[pl.ds(pl.multiple_of(b // 2 * 2 * rows, 2 * rows), 2 * rows), :].astype(F32)
            xs.append(jnp.where(b % 2 == 1, two[rows:], two[:rows]))
            own = (block_lane == b) & valid
            column = jnp.sum(jnp.where(own, coefs, 0.0), axis=1, keepdims=True)
            diff = diff_ref[...] - off_ref[b]
            band = jnp.zeros(diff.shape, F32)
            for t in range(6):
                band = jnp.where(diff == t, column[t : t + 1, :], band)
            bands.append(band)
            slot = jnp.where(valid, dest_ref[b] % blocks, -1).astype(F32)
            weight = jnp.sum(jnp.where(own, wgt_ref[...], 0.0), axis=1, keepdims=True)
            note = jnp.where(lane == 0, slot, 0.0)
            for i, part in enumerate(three(jnp.broadcast_to(weight, (rows, LANE)))):
                note = jnp.where(lane == i + 1, part, note)
            noted[group] = jnp.where(line == rank, note, noted.get(group, 0.0))
        x16 = jnp.concatenate(xs, axis=0).astype(BF)
        padded = jnp.concatenate([zero, x16, zero], axis=1)
        windows = jnp.concatenate(
            [padded[:, LANE * t : LANE * (t + 2)] for t in range(tiles + 1)], axis=0
        )
        band = jnp.concatenate(bands, axis=1).astype(BF)
        band = jnp.concatenate([jnp.zeros((ROW0, 2 * LANE), BF), band], axis=0)
        made = dot(windows, band)

        def piece(i):
            at = made[2 * rows * i : 2 * rows * (i + 1)]
            return at[:rows, :LANE], at[rows:, LANE:]

        tops, bottoms = [list(half) for half in zip(*(piece(t) for t in range(tiles)))]
        last = piece(tiles)
        tops[0] = jnp.where(lane < SHIFT, last[0], tops[0])
        bottoms[0] = jnp.where(lane < SHIFT, last[1], bottoms[0])
        (group0, rank0), (group1, rank1) = slots
        if group0 == group1:
            for t in range(tiles):
                put(group0, rank0 // 2 * tiles + t, tops[t], bottoms[t])
        else:
            half = tiles // 2
            for group, pieces in ((group0, tops), (group1, bottoms)):
                for t in range(half):
                    put(group, cap // 2 * tiles + t, pieces[t], pieces[t + half])

    def put(group, tile, top, bottom):
        made_ref[order.index(group), :, LANE * tile : LANE * (tile + 1)] = jnp.concatenate(
            [top, bottom], axis=0
        ).astype(BF)

    sends = [pltpu.make_async_copy(made_ref.at[i], outs[i], sems.at[6 + i]) for i in range(len(order))]
    for at in range(0, len(order), 2):
        two = order[at : at + 2]
        for group in two:
            for rank in range(0, cap - 1, 2):
                one_pair([(group, rank), (group, rank + 1)])
        if cap % 2:
            one_pair([(two[0], cap - 1), (two[1], cap - 1)])
        for group in two:
            put(group, made_ref.shape[2] // LANE - 1, noted[group], fit_note)
        for i in range(2):
            sends[at + i].start()
    for send in sends:
        send.wait()


def message_shape(cap, rows, width):
    tiles = width // LANE
    return 2 * rows, LANE * (cap // 2 * tiles + cap % 2 * (tiles // 2) + 1)


def resample(exposure, dest, offset, shift, weight, fit, peers, cap, order):
    rows_dev, width = exposure.shape
    blocks = dest.shape[0]
    rows = rows_dev // blocks
    hbm = pl.BlockSpec(memory_space=pl.ANY)
    return pl.pallas_call(
        functools.partial(resample_kernel, cap, peers, order, len(fit)),
        in_specs=[hbm] * (5 + len(fit)),
        out_specs=[hbm] * len(order),
        out_shape=[jax.ShapeDtypeStruct(message_shape(cap, rows, width), BF)] * len(order),
        scratch_shapes=[
            pltpu.SMEM((blocks,), jnp.int32),
            pltpu.SMEM((blocks,), jnp.int32),
            pltpu.SMEM((peers * cap,), jnp.int32),
            pltpu.SMEM((peers,), jnp.int32),
            pltpu.VMEM((1, blocks), F32),
            pltpu.VMEM((1, blocks), F32),
            pltpu.VMEM((rows_dev, width), BF),
            pltpu.VMEM((len(order),) + message_shape(cap, rows, width), BF),
            pltpu.VMEM((2 * LANE - ROW0, LANE), jnp.int32),
            pltpu.VMEM((1, LANE), F32),
            pltpu.SemaphoreType.DMA((6 + len(order),)),
        ],
        compiler_params=pltpu.CompilerParams(vmem_limit_bytes=LATE_VMEM if fit else EARLY_VMEM),
        name="resample",
    )(dest, offset, shift.reshape(1, blocks), weight.reshape(1, blocks), exposure, *fit)


def gauss_band(shape, rows_axis, width, total):
    u = lax.broadcasted_iota(jnp.int32, shape, 1 - rows_axis)
    u = u - lax.broadcasted_iota(jnp.int32, shape, rows_axis) - 1
    at = (u - HALF).astype(F32)
    value = jnp.exp(-(at * at) / (2.0 * width * width)) / total
    return jnp.where((u >= 0) & (u < TAPS), value, 0.0).astype(BF)


def tables_kernel(width_ref, band_ref, inner_ref, edge_ref):
    inner, rows_dev = inner_ref.shape[1:]
    edge_ref[...] = jnp.zeros(edge_ref.shape, BF)
    for k in range(BASES):
        width = jnp.full((8, LANE), width_ref[k], F32)[:1, :1]
        tap = lax.broadcasted_iota(jnp.int32, (1, LANE), 1)
        at = (tap - HALF).astype(F32)
        each = jnp.where(tap < TAPS, jnp.exp(-(at * at) / (2.0 * width * width)), 0.0)
        total = jnp.sum(each, axis=1, keepdims=True)
        band_ref[:, LANE * k : LANE * (k + 1)] = gauss_band((2 * LANE, LANE), 1, width, total)
        inner_ref[k] = gauss_band((inner, rows_dev), 0, width, total)
        strip = gauss_band((EDGE, 3 * EDGE), 0, width, total)
        none = jnp.zeros(strip.shape, BF)
        edge_ref[2 * EDGE * k : 2 * EDGE * k + EDGE, :] = jnp.concatenate([strip, none], axis=1)
        edge_ref[2 * EDGE * k + EDGE : 2 * EDGE * (k + 1), :] = jnp.concatenate([none, strip], axis=1)


def tables(basis_width, rows_dev):
    sd = lambda *shape: jax.ShapeDtypeStruct(shape, BF)
    return pl.pallas_call(
        tables_kernel,
        in_specs=[pl.BlockSpec(memory_space=pltpu.SMEM)],
        out_shape=[
            sd(2 * LANE, BASES * LANE),
            sd(BASES, rows_dev - 2 * EDGE, rows_dev),
            sd(2 * EDGE * BASES, 6 * EDGE),
        ],
        compiler_params=pltpu.CompilerParams(vmem_limit_bytes=SMALL_VMEM),
        name="tables",
    )(basis_width)


def split_rows(groups, cap, tiles, first, count):
    parts = []
    at = [LANE * (pair * tiles + first) for pair in range(cap // 2)]
    if at:
        pairs = [g[:, a : a + LANE * count] for g in groups for a in at]
        parts.append(jnp.concatenate(pairs, axis=0))
    if cap % 2:
        half, base = tiles // 2, cap // 2 * tiles
        upper, lower = max(0, min(half, first + count) - first), max(0, first + count - max(first, half))
        alone = []
        for g in groups:
            rows = g.shape[0] // 2
            pieces = []
            if upper:
                a = LANE * (base + first)
                pieces.append(g[:, a : a + LANE * upper].astype(F32)[:rows])
            if lower:
                a = LANE * (base + max(first, half) - half)
                pieces.append(g[:, a : a + LANE * lower].astype(F32)[rows:])
            alone.append(jnp.concatenate(pieces, axis=1))
        parts.append(jnp.concatenate(alone, axis=0).astype(BF))
    return parts


def plan_slots(notes, rows, rows_dev, cap, peers):
    slots, size = rows_dev // rows, 2 * rows
    fit = sum(
        notes[size * g + rows + i : size * g + rows + i + 1].astype(F32)
        for g in range(0, peers, 2)
        for i in range(3)
    )
    spread = lambda at: lax.dot_general(
        notes, jnp.where(at, 1.0, 0.0).astype(BF), (((0,), (0,)), ((), ())), preferred_element_type=F32
    )
    source = lax.broadcasted_iota(jnp.int32, (size * peers, 1), 0)
    row = lax.broadcasted_iota(jnp.int32, (rows_dev, 1), 0)
    even = cap // 2 * 2
    places, cover = [], 0.0
    for first, held in ((0, even), (even, cap - even)):
        if not held:
            continue
        lane = lax.broadcasted_iota(jnp.int32, (1, peers * held * rows), 1)
        block = lane // rows
        told = spread(source == block // held * size + first + block % held)
        match = (told[:1].astype(jnp.int32) == row // rows) & (lane % rows == row % rows)
        places.append(jnp.where(match, 1.0, 0.0).astype(BF))
        weight = told[1:2] + told[2:3] + told[3:4]
        cover = cover + jnp.sum(jnp.where(match, weight, 0.0), axis=1, keepdims=True)
    scale = jnp.broadcast_to(1.0 / jnp.maximum(cover, 1.0), (rows_dev, LANE))
    index = lax.broadcasted_iota(jnp.int32, (1, slots), 1)
    mine = (notes[:, :1].astype(F32).astype(jnp.int32) == index) & (source % size < cap)
    lined = spread(mine)
    return places, scale, lined[1:2] + lined[2:3] + lined[3:4], fit


def coadd_kernel(peers, cap, rows, chunk, *refs):
    groups = refs[:peers]
    image_ref, inward_ref, outward_ref, cover_ref, fit_ref = refs[peers:]
    rows_dev, width = image_ref.shape
    tiles = width // LANE
    odd = lax.axis_index(BOTH) % 2 == 1
    notes = jnp.concatenate([g[:, g.shape[1] - LANE :] for g in groups], axis=0)
    places, scale, cover, fit = plan_slots(notes, rows, rows_dev, cap, peers)
    cover_ref[...] = cover
    fit_ref[...] = fit
    for at in range(0, width, chunk):
        cols = slice(at, at + chunk)
        value = None
        for part, place in zip(split_rows(groups, cap, tiles, at // LANE, chunk // LANE), places):
            sums = dot(place, part)
            value = sums if value is None else value + sums
        value = (value * scale[:, :1]).astype(BF)
        image_ref[:, cols] = value
        top, bottom = value[:EDGE], value[rows_dev - EDGE :]
        inward_ref[:, cols] = jnp.where(odd, top, bottom)
        outward_ref[:, cols] = jnp.where(odd, bottom, top)


def coadd(groups, cap, rows_dev, rows, width):
    peers = len(groups)
    sd = jax.ShapeDtypeStruct
    vmem = pl.BlockSpec(memory_space=pltpu.VMEM)
    return pl.pallas_call(
        functools.partial(coadd_kernel, peers, cap, rows, CHUNK2),
        in_specs=[vmem] * peers,
        out_specs=[vmem] * 5,
        out_shape=[
            sd((rows_dev, width), BF),
            sd((EDGE, width), BF),
            sd((EDGE, width), BF),
            sd((1, rows_dev // rows), F32),
            sd((1, LANE), F32),
        ],
        compiler_params=pltpu.CompilerParams(vmem_limit_bytes=SMALL_VMEM),
        name="coadd",
    )(*groups)


def row_position(base, count, all_rows):
    at = (base + lax.broadcasted_iota(jnp.int32, (count, 1), 0)).astype(F32)
    return 2.0 * at / (all_rows - 1) - 1.0


def col_position(first, count, col_count):
    at = (first + lax.broadcasted_iota(jnp.int32, (1, count), 1)).astype(F32)
    return 2.0 * at / (col_count - 1) - 1.0


def field(fit_ref, k, y, xx):
    c = lambda i: fit_ref[0, FIT0 + NPOLY * k + i]
    return (c(0) + c(2) * y + c(5) * y * y) + (c(1) + c(4) * y) * xx + c(3) * (xx * xx)


def lane_of(value):
    return lax.broadcasted_iota(jnp.int32, (1, value.shape[1]), 1)


def blank(value, keep):
    return jnp.where(keep, value, jnp.zeros_like(value))


def tile_windows(value, tiles):
    return jnp.concatenate([value[:, LANE * t : LANE * (t + 2)] for t in range(tiles)], axis=0)


def inner_rows(image, first, start, fit_ref, band_ref, inner_ref, all_rows, col_count):
    rows_dev, width = image.shape
    inner = rows_dev - 2 * EDGE
    tiles = width // LANE - 1
    smooth = dot(tile_windows(image, tiles), band_ref[...]).astype(BF)
    y = row_position(start + EDGE, inner, all_rows)
    xx = col_position(first, LANE * tiles, col_count)
    total = None
    for k in range(BASES):
        part = jnp.concatenate(
            [smooth[rows_dev * t : rows_dev * (t + 1), LANE * k : LANE * (k + 1)] for t in range(tiles)],
            axis=1,
        )
        term = field(fit_ref, k, y, xx) * dot(inner_ref[k], part)
        total = term if total is None else total + term
    return total.astype(BF)


def inner_kernel(
    all_rows, chunk, start_ref, fit_ref, image_ref, band_ref, inner_ref, out_ref, made_ref, sems
):
    rows_dev, col_count = image_ref.shape
    inner = rows_dev - 2 * EDGE
    sends = []
    for at in range(0, col_count, chunk):
        x = image_ref[:, at : at + chunk]
        head, tail = x[:, :LANE], image_ref[:, (at + chunk) % col_count :][:, :LANE]
        if at == 0:
            head = blank(head, lane_of(head) >= SHIFT)
        if at + chunk == col_count:
            tail = blank(tail, lane_of(tail) < SHIFT)
        image = jnp.concatenate([head, x[:, LANE:], tail], axis=1)
        value = inner_rows(
            image, at, start_ref[0], fit_ref, band_ref, inner_ref, all_rows, col_count
        )
        slot = len(sends) % 2
        if len(sends) >= 2:
            sends[-2].wait()
        made_ref[slot] = value
        send = pltpu.make_async_copy(
            made_ref.at[slot], out_ref.at[pl.ds(EDGE, inner), pl.ds(at, chunk)], sems.at[slot]
        )
        send.start()
        sends.append(send)
    for send in sends[-2:]:
        send.wait()


def whole_of(v):
    return pl.BlockSpec(v.shape, lambda i: (0,) * v.ndim)


def match_inner(image, start, fit, band, inner, all_rows):
    rows_dev, col_count = image.shape
    chunk = CHUNK3
    smem = pl.BlockSpec(memory_space=pltpu.SMEM)
    vmem = pl.BlockSpec(memory_space=pltpu.VMEM)
    return pl.pallas_call(
        functools.partial(inner_kernel, all_rows, chunk),
        in_specs=[smem, smem, vmem, vmem, vmem],
        out_specs=pl.BlockSpec(memory_space=pl.ANY),
        out_shape=jax.ShapeDtypeStruct((rows_dev, col_count), BF),
        scratch_shapes=[
            pltpu.VMEM((2, rows_dev - 2 * EDGE, chunk), BF),
            pltpu.SemaphoreType.DMA((2,)),
        ],
        compiler_params=pltpu.CompilerParams(vmem_limit_bytes=MATCH_VMEM),
        name="match_inner",
    )(start, fit, image, band, inner)


def edge_kernel(
    all_rows, rows_dev, start_ref, fit_ref, inward_ref, image_ref, outward_ref, band_ref,
    edge_ref, old_ref, out_ref, made_ref, sems,
):
    col_count = made_ref.shape[1]
    tiles = col_count // LANE
    odd = lax.axis_index(BOTH) % 2 == 1
    inward, outward = inward_ref[...], outward_ref[...]
    above, below = jnp.where(odd, inward, outward), jnp.where(odd, outward, inward)
    top, bottom = image_ref[: 2 * EDGE], image_ref[rows_dev - 2 * EDGE :]
    x = jnp.concatenate([above, top, bottom, below], axis=0)
    rowconv = dot(edge_ref[...], x).astype(BF)
    head = rowconv[:, :LANE]
    rowconv = jnp.concatenate(
        [blank(head, lane_of(head) >= SHIFT), rowconv[:, LANE:], blank(head, lane_of(head) < SHIFT)],
        axis=1,
    )
    y = jnp.concatenate(
        [row_position(start_ref[0] + at, EDGE, all_rows) for at in (0, rows_dev - EDGE)], axis=0
    )
    both = 2 * EDGE
    parts = [
        dot(tile_windows(rowconv[both * k : both * (k + 1)], tiles), band_ref[:, LANE * k : LANE * (k + 1)])
        for k in range(BASES)
    ]
    for t in range(tiles):
        xx = col_position(LANE * t, LANE, col_count)
        total = None
        for k in range(BASES):
            term = field(fit_ref, k, y, xx) * parts[k][both * t : both * (t + 1)]
            total = term if total is None else total + term
        made_ref[:, LANE * t : LANE * (t + 1)] = total.astype(BF)
    copies = [
        pltpu.make_async_copy(
            made_ref.at[pl.ds(EDGE * i, EDGE)], out_ref.at[pl.ds(at, EDGE)], sems.at[i]
        )
        for i, at in enumerate((0, rows_dev - EDGE))
    ]
    for copy in copies:
        copy.start()
    for copy in copies:
        copy.wait()


def match_edges(matched, image, halos, start, fit, band, edge, all_rows):
    rows_dev, col_count = matched.shape
    smem = pl.BlockSpec(memory_space=pltpu.SMEM)
    vmem = pl.BlockSpec(memory_space=pltpu.VMEM)
    hbm = pl.BlockSpec(memory_space=pl.ANY)
    return pl.pallas_call(
        functools.partial(edge_kernel, all_rows, rows_dev),
        in_specs=[smem, smem] + [vmem] * 5 + [hbm],
        out_specs=hbm,
        out_shape=jax.ShapeDtypeStruct(matched.shape, BF),
        scratch_shapes=[pltpu.VMEM((2 * EDGE, col_count), BF), pltpu.SemaphoreType.DMA((2,))],
        input_output_aliases={7: 0},
        compiler_params=pltpu.CompilerParams(vmem_limit_bytes=SMALL_VMEM),
        name="match_edges",
    )(start, fit, halos[0], image, halos[1], band, edge, matched)


def shards(
    exposure, block_dest, band_offset, col_shift, block_weight, basis_width, kernel_fit, fit_owner
):
    rows_dev, col_count = exposure.shape
    blocks = block_dest.shape[0]
    peers = lax.axis_size("patch")
    dets = lax.axis_size("det")
    devices = lax.axis_size(BOTH)
    cap = blocks // peers + 1
    me = lax.axis_index(BOTH)
    all_rows = rows_dev * devices
    start = jnp.full((1,), me * rows_dev, jnp.int32)
    send = lambda group, s: lax.ppermute(
        group, "patch", [(i, i ^ s) for i in range(peers)]
    )
    order = sorted(range(peers), key=lambda s: (s % 2 == 0, -s))
    early_order = order[:2]
    late_order = sorted(order[2:], key=lambda s: -s)
    partner_fit = lax.ppermute(kernel_fit, "patch", [(i, i ^ 1) for i in range(peers)])
    source = (exposure, block_dest, band_offset, col_shift, block_weight)
    early = resample(*source, [], peers, cap, early_order)
    groups = {s: send(group, s) for s, group in zip(early_order, early)}
    source, early, fit, partner_fit = lax.optimization_barrier(
        (source, early, kernel_fit, partner_fit)
    )
    owner = fit_owner[0]
    partner = me ^ 1
    fit = jnp.where(me == owner, fit, 0.0) + jnp.where(partner == owner, partner_fit, 0.0)
    fit = fit.reshape(1, BASES * NPOLY)
    span = 1
    while span < dets:
        fit = fit + lax.ppermute(fit, "det", [(i, i ^ span) for i in range(dets)])
        span *= 2
    fit = jnp.pad(fit, ((0, 0), (0, LANE - BASES * NPOLY)))
    fit = jnp.roll(fit, FIT0, axis=1)
    late = resample(*source, [fit], peers, cap, late_order)
    for s, group in zip(late_order, late):
        groups[s] = send(group, s) if s else group
    late, basis_width = lax.optimization_barrier((late, basis_width))
    band, inner, edge = tables(basis_width, rows_dev)
    groups = [groups[s] for s in range(peers)]
    groups, band, inner, edge = lax.optimization_barrier((groups, band, inner, edge))
    image, inward, outward, cover, fit = coadd(groups, cap, rows_dev, rows_dev // blocks, col_count)
    even = [(i, i ^ 1) for i in range(devices)]
    odd = [(i, j) for j in range(2, devices, 2) for i, j in ((j, j - 1), (j - 1, j))]
    halos = (lax.ppermute(inward, BOTH, even), lax.ppermute(outward, BOTH, odd))
    matched = match_inner(image, start, fit, band, inner, all_rows)
    matched = match_edges(matched, image, halos, start, fit, band, edge, all_rows)
    return matched, cover.reshape(blocks)


def solution(mesh):
    in_specs = (
        P(BOTH, None),
        P(BOTH),
        P(BOTH),
        P(BOTH),
        P(BOTH),
        P(),
        P(BOTH, None, None),
        P(),
    )
    out_specs = (P(BOTH, None), P(BOTH))
    return jax.shard_map(shards, mesh=mesh, in_specs=in_specs, out_specs=out_specs, check_vma=False)
```
